32 devices in a mesh: atoms: 8 (over y, x, core), grid: 4 (over z).
Axes of the slice: x: 2, y: 2, z: 4, core: 2. Of those that a mesh axis runs over, the one named last changes fastest.
Arguments:
- column_blocks: bfloat16 [256, 32, 256], P('atoms'), may hold values from -1 to 1
- onsite: bfloat16 [256, 256], P('atoms'), may hold values from -1 to 1
- neighbor_ids: int32 [256, 32], P('atoms'), may hold values from 0 to 255, as said below
- task_atoms: int32 [128, 32], P(('atoms', 'grid')), may hold values from 0 to 255, as said below
- chem_shift: float32 [128], P(('atoms', 'grid')), may hold values from -0.6 to 0.6
- basis_values: bfloat16 [128, 512, 1024], P(('atoms', 'grid')), may hold values from -0.59765625 to 0.59765625
- box_start: int32 [128], P(('atoms', 'grid')), may hold values from 0 to 252
- box_row: int32 [128], P(('atoms', 'grid')), may hold values from 0 to 16
- box_col: int32 [128], P(('atoms', 'grid')), may hold values from 0 to 112
Outputs:
- density_cols: bfloat16 [128, 512, 128], P(('atoms', 'grid'))
- rho: float32 [256, 32, 128], P('grid')
The draws below stay inside these ranges and needn't reach their ends.
Inputs may be any that keep to these rules, and one draw needn't show every extreme that they name: `task_atoms`: row a of a device's block of 4 tasks, task t, names 8 atoms from each of 4 devices' columns. The atoms named by one device's tasks are all different; at most 16 of them lie in one device's columns, and some device's columns hold exactly 16 of them. `neighbor_ids`: an atom's 32 entries are different atoms, never the atom itself.
All inputs are finite; a program needn't handle non-finite values. Where the reference program divides by a largest or mean magnitude, that divisor is 1e-20 or more.
Results may differ from the reference program's by a relative error of at most 0.007.
Values may be sent and summed in bfloat16 or wider, within the bound.
No kernel may reach another device: no remote copies, remote signals or barrier semaphores. Data moves between devices by JAX's collectives and lax.ppermute only.
A program may use at most 64 MiB of HBM per device.

```python
import math
import jax
import jax.numpy as jnp
import numpy as np
from jax import lax

BS = 16
KNB = 32
PICK = 8
SPAN = 4
ITERS = 3
BOXP = 4
BOX_ROWS = 16
BOX_COLS = 16
GRID_ROWS = 32
GRID_COLS = 128
PL_SLAB = 64
ATOM_DEV = 32
TASK_DEV = 4
NNB = 32
ORDER = 512
CENTRAL = 128
BOX_POINTS = 1024
NA = 256
TASKS = 128
PLANES = 256
N_ATOMS = 8
N_GRID = 4


def draw_column_blocks(key, part):
    scale_key, sign_key, level_key, spread_key, keep_key = jax.random.split(jax.random.fold_in(key, 53), 5)
    scale = jnp.exp(jax.random.uniform(scale_key, (NA, KNB, 1, 1), jnp.float32, math.log(0.003), 0.0))
    signs = jnp.where(jax.random.bernoulli(sign_key, 0.5, (NA, KNB, BS)), 1.0, -1.0).astype(jnp.float32)
    levels = jax.random.uniform(level_key, (NA, KNB, BS), jnp.float32, 0.5, 1.0)
    spread = jnp.clip(0.1 * jax.random.normal(spread_key, (NA, KNB, BS, BS), jnp.float32), -0.4, 0.4)
    keep = jax.random.bernoulli(keep_key, 0.3, (NA, KNB, BS, BS))
    identity = jnp.eye(BS, dtype=jnp.float32)
    diagonal_part = identity[None, None, :, :] * (signs * levels)[:, :, :, None]
    off_part = (1.0 - identity)[None, None, :, :] * jnp.where(keep, spread, 0.0)
    blocks = scale * (diagonal_part + off_part)
    return blocks.reshape(NA, KNB, BS * BS).astype(jnp.bfloat16)


def draw_onsite(key, part):
    first_key, second_key, third_key = jax.random.split(jax.random.fold_in(key, 37), 3)
    coupling = jnp.clip(0.025 * jax.random.normal(first_key, (NA, BS, BS), jnp.float32), -0.1, 0.1)
    magnitude = jax.random.uniform(second_key, (NA, BS), jnp.float32, 0.2, 0.6)
    upward = jax.random.bernoulli(third_key, 0.5, (NA, BS))
    levels = jnp.where(upward, magnitude, -magnitude)
    identity = jnp.eye(BS, dtype=jnp.float32)[None, :, :]
    matrix_full = (1.0 - identity) * coupling + levels[:, :, None] * identity
    return matrix_full.reshape(NA, BS * BS).astype(jnp.bfloat16)


def draw_neighbor_ids(key, part):
    half_window = (ATOM_DEV - 1) // 2
    offsets = np.array([(dq, dl) for dq in range(1 - SPAN, SPAN) for dl in range(-half_window, half_window + 1) if (dq, dl) != (0, 0)], dtype=np.int32)
    keys_all = jax.random.split(jax.random.fold_in(key, 11), NA)
    chosen = jax.vmap(lambda single: jax.random.permutation(single, offsets.shape[0])[:KNB])(keys_all)
    shift_dev = jnp.asarray(offsets[:, 0])[chosen]
    shift_local = jnp.asarray(offsets[:, 1])[chosen]
    atom_index = jnp.arange(NA, dtype=jnp.int32)
    holder = atom_index // ATOM_DEV
    within = atom_index % ATOM_DEV
    result = (holder[:, None] + shift_dev) % N_ATOMS * ATOM_DEV + (within[:, None] + shift_local) % ATOM_DEV
    return result.astype(jnp.int32)


def draw_task_atoms(key, part):
    device_count = TASKS // TASK_DEV
    first_key, second_key = jax.random.split(jax.random.fold_in(key, 23))
    base_dev = jax.random.randint(first_key, (device_count,), 0, N_ATOMS)
    base_local = jax.random.randint(second_key, (device_count,), 0, ATOM_DEV)
    task_index = jnp.arange(TASK_DEV, dtype=jnp.int32)[None, :, None, None]
    span_index = jnp.arange(SPAN, dtype=jnp.int32)[None, None, :, None]
    pick_index = jnp.arange(PICK, dtype=jnp.int32)[None, None, None, :]
    holder = (base_dev[:, None, None, None] + SPAN * task_index + span_index) % N_ATOMS
    within = (base_local[:, None, None, None] + PICK * task_index + pick_index) % ATOM_DEV
    result = holder * ATOM_DEV + within
    return result.reshape(TASKS, NNB).astype(jnp.int32)


def touch_ends(entries, rng, low, high):
    place = [jax.random.randint(jax.random.fold_in(rng, axis), (), 0, length) for axis, length in enumerate(entries.shape)]
    main_axis = entries.shape.index(max(entries.shape))
    beside = place[:main_axis] + [(place[main_axis] + 1) % entries.shape[main_axis]] + place[main_axis + 1:]
    return entries.at[tuple(place)].set(low).at[tuple(beside)].set(high)


def steps_of(own_key, extent, cuts, smallest, largest):
    def one(axis_at, blocks):
        draws = jax.random.uniform(jax.random.fold_in(jax.random.fold_in(own_key, 6), axis_at), (blocks,), jnp.float32, smallest / len(cuts), largest / len(cuts))
        return jnp.repeat(jnp.exp(draws), extent[axis_at] // blocks).reshape((-1,) + (1,) * (len(extent) - axis_at - 1))

    loudness = one(*cuts[0])
    for cut in cuts[1:]:
        loudness = loudness * one(*cut)
    return loudness


def scatter_about(stream_key, shape, scale, limit, pieces=(), held_as=jnp.bfloat16):
    factor_of = steps_of(stream_key, shape, pieces, -0.22, 0.18) if pieces else 1.0
    entries = jax.random.normal(stream_key, shape, jnp.float32) * scale * factor_of
    return jnp.minimum(jnp.maximum(entries, -limit), limit).astype(held_as)


def setup_inputs(seed: int = 0) -> dict:
    seeds = jax.random.split(jax.random.key(seed), 10)
    column_blocks = draw_column_blocks(jax.random.fold_in(seeds[9], 71), 0)
    onsite = draw_onsite(jax.random.fold_in(seeds[9], 71), 0)
    neighbor_ids = draw_neighbor_ids(jax.random.fold_in(seeds[9], 71), 0)
    task_atoms = draw_task_atoms(jax.random.fold_in(seeds[9], 71), 0)
    chem_shift = jnp.clip(jax.random.uniform(seeds[4], (TASKS,), jnp.float32, -0.6, 0.6) * steps_of(seeds[4], (TASKS,), ((0, 32),), -0.4, 0.0), -0.6, 0.6)
    basis_values = scatter_about(seeds[5], (TASKS, ORDER, BOX_POINTS), 0.1, 0.59765625, ((0, 32),))
    box_start = touch_ends(jax.random.randint(seeds[6], (TASKS,), 0, PLANES - BOXP + 1), jax.random.fold_in(seeds[6], 1), 0, PLANES - BOXP).astype(jnp.int32)
    box_row = touch_ends(jax.random.randint(seeds[7], (TASKS,), 0, GRID_ROWS - BOX_ROWS + 1), jax.random.fold_in(seeds[7], 1), 0, GRID_ROWS - BOX_ROWS).astype(jnp.int32)
    box_col = touch_ends(jax.random.randint(seeds[8], (TASKS,), 0, GRID_COLS - BOX_COLS + 1), jax.random.fold_in(seeds[8], 1), 0, GRID_COLS - BOX_COLS).astype(jnp.int32)
    return {"column_blocks": column_blocks, "onsite": onsite, "neighbor_ids": neighbor_ids, "task_atoms": task_atoms, "chem_shift": chem_shift, "basis_values": basis_values, "box_start": box_start, "box_row": box_row, "box_col": box_col}


exact_mode = lax.Precision.HIGHEST


def assemble(columns_in, onsite_in, links_in, members, offset):
    count = members.shape[0]
    matched = (links_in[None, :, :] == members[:, None, None]).astype(jnp.float32)
    blocks = columns_in.astype(jnp.float32).reshape(count, KNB, BS, BS)
    coupled = jnp.einsum("ijk,jkab->iajb", matched, blocks, precision=exact_mode)
    diagonal_part = jnp.einsum("ij,jab->iajb", jnp.eye(count, dtype=jnp.float32), onsite_in.astype(jnp.float32).reshape(count, BS, BS), precision=exact_mode)
    whole = (coupled + diagonal_part).reshape(count * BS, count * BS)
    return 0.5 * (whole + whole.T) - offset * jnp.eye(count * BS, dtype=jnp.float32)


def sign_columns(matrix):
    order_size = matrix.shape[0]
    identity = jnp.eye(order_size, dtype=jnp.float32)
    bound = jnp.max(jnp.sum(jnp.abs(matrix), axis=1)) + 1e-6
    iterate = (matrix / bound).astype(jnp.bfloat16)
    for iteration in range(ITERS - 1):
        squared = jnp.dot(iterate, iterate, preferred_element_type=jnp.float32)
        factor = (1.5 * identity - 0.5 * squared).astype(jnp.bfloat16)
        iterate = jnp.dot(iterate, factor, preferred_element_type=jnp.float32).astype(jnp.bfloat16)
    squared = jnp.dot(iterate, iterate[:, :CENTRAL], preferred_element_type=jnp.float32)
    factor = (1.5 * identity[:, :CENTRAL] - 0.5 * squared).astype(jnp.bfloat16)
    last_product = jnp.dot(iterate, factor, preferred_element_type=jnp.float32)
    return (0.5 * (identity[:, :CENTRAL] - last_product)).astype(jnp.bfloat16)


def collocate(density, basis_rows):
    weights = lax.dot_general(density, basis_rows, (((0,), (0,)), ((), ())), preferred_element_type=jnp.float32)
    values = jnp.sum(weights * basis_rows[:CENTRAL].astype(jnp.float32), axis=0)
    return values.reshape(BOXP, BOX_ROWS, BOX_COLS)


def reference(column_blocks, onsite, neighbor_ids, task_atoms, chem_shift, basis_values, box_start, box_row, box_col):
    def one_task(members):
        atom_ids, offset, basis_rows = members
        matrix = assemble(column_blocks[atom_ids], onsite[atom_ids], neighbor_ids[atom_ids], atom_ids, offset)
        density = sign_columns(matrix)
        return density, collocate(density, basis_rows)

    density_cols, boxes = lax.map(one_task, (task_atoms, chem_shift, basis_values))

    def add_box(index, grid_now):
        corner = (box_start[index].astype(jnp.int32), box_row[index].astype(jnp.int32), box_col[index].astype(jnp.int32))
        current = lax.dynamic_slice(grid_now, corner, (BOXP, BOX_ROWS, BOX_COLS))
        return lax.dynamic_update_slice(grid_now, current + boxes[index], corner)

    empty_grid = jnp.zeros((PL_SLAB * N_GRID, GRID_ROWS, GRID_COLS), jnp.float32)
    rho = lax.fori_loop(0, TASKS, add_box, empty_grid)
    return density_cols, rho
```

```python
import functools

import jax
import jax.numpy as jnp
from jax import lax
from jax.experimental import pallas as pl
from jax.experimental.pallas import tpu as pltpu
from jax.sharding import PartitionSpec as P

BS = 16
ITERS = 3
BOXP = 4
BOX_ROWS = 16
BOX_COLS = 16
GRID_ROWS = 32
GRID_COLS = 128
PL_SLAB = 64
CENTRAL = 128

LOW = 8
LANES = 128


def doubled(value, axis, size, pairs):
    for step in pairs:
        other = lax.ppermute(value, axis, [(i, i ^ step) for i in range(size)])
        value = jnp.concatenate([value, other], axis=0)
    return value


def power_of_two(size):
    return size & (size - 1) == 0


def gather_everywhere(value):
    for axis in ("grid", "atoms"):
        size = lax.axis_size(axis)
        if power_of_two(size):
            steps = [1 << bit for bit in range(size.bit_length() - 1)][::-1]
            value = doubled(value, axis, size, steps)
        else:
            value = lax.all_gather(value, axis, axis=0, tiled=True)
    return value


def gather_columns(packed, holders):
    if holders < 2 or not power_of_two(holders):
        whole = lax.all_gather(packed, "atoms", axis=0)
        return [whole[i] for i in range(holders)], lambda holder: holder
    stages = holders.bit_length() - 2
    half = holders // 2

    def bit_of(device, stage):
        return 2 << (stages - 1 - stage if device & 1 else stage)

    pieces = [packed]
    for stage in range(stages):
        pairs = [(i, i ^ bit_of(i, stage)) for i in range(holders)]
        pieces = pieces + [lax.ppermute(piece, "atoms", pairs) for piece in pieces]
    swap = [(i, i ^ 1) for i in range(holders)]
    pieces = pieces + [lax.ppermute(piece, "atoms", swap) for piece in pieces]

    def slot(holder):
        apart = holder ^ lax.axis_index("atoms")
        plain = apart >> 1
        turned = sum((((plain >> bit) & 1) << (stages - 1 - bit) for bit in range(stages)), 0 * plain)
        return (apart & 1) * half + jnp.where(holder & 1 == 1, turned, plain)

    return pieces, slot


def iota(shape, axis):
    return lax.broadcasted_iota(jnp.int32, shape, axis)


def nn(left, right):
    return jnp.dot(left, right, preferred_element_type=jnp.float32)


def nt(left, right):
    return lax.dot_general(left, right, (((1,), (1,)), ((), ())), preferred_element_type=jnp.float32)


def density_kernel(
    holders,
    atoms_here,
    links,
    place_ref,
    shift_ref,
    slot_col_ref,
    member_col_ref,
    basis_ref,
    *rest,
):
    pieces = rest[:holders]
    density_ref, box_ref, cols, onsites, idents, ids_all, onsite_all, product, matrix, sems = rest[holders:]
    half = jnp.bfloat16
    task = pl.program_id(0)
    set_size = member_col_ref.shape[1]
    order = set_size * BS
    area = BS * BS
    block_rows = atoms_here * links
    groups = set_size // LOW

    @pl.when(task == 0)
    def _():
        copies = []
        for number, piece in enumerate(pieces):
            copies.append(
                pltpu.make_async_copy(
                    piece.at[pl.ds(0, block_rows)], cols.at[pl.ds(number * block_rows, block_rows)], sems.at[0, number]
                )
            )
            copies.append(
                pltpu.make_async_copy(
                    piece.at[pl.ds(block_rows, atoms_here)],
                    onsites.at[pl.ds(number * atoms_here, atoms_here)],
                    sems.at[1, number],
                )
            )
            copies.append(
                pltpu.make_async_copy(
                    piece.at[pl.ds(block_rows + atoms_here, atoms_here)],
                    idents.at[pl.ds(number * atoms_here, atoms_here)],
                    sems.at[2, number],
                )
            )
        for copy in copies:
            copy.start()
        for copy in copies:
            copy.wait()
        count = slot_col_ref.shape[0]
        chosen = (slot_col_ref[...] == iota((count, holders * atoms_here), 1)).astype(jnp.float32).astype(half)
        onsite_all[...] = nn(chosen, onsites[...])
        raw = nn(chosen, idents[...]).astype(half)
        source, target = iota((area, LOW * links), 0), iota((area, LOW * links), 1) % links
        spread = jnp.where(source == target, 1.0, jnp.where(source == links + target, 256.0, 0.0)).astype(half)
        ids_all[...] = nn(raw, spread)

    source, target = iota((area, area), 0), iota((area, area), 1)
    wanted = ((target // LANES) * LOW + target % LOW) * BS + (target % LANES) // LOW
    reorder = (source == wanted).astype(jnp.float32).astype(half)

    member = member_col_ref[0]
    lane_owner = iota((LOW, LOW * links), 1) // links
    own = lane_owner == iota((LOW, LOW * links), 0)
    owner_wide = iota((set_size, LOW * links), 1) // links
    lane = iota((set_size, LANES), 1)
    for group in range(groups):
        base = pl.multiple_of(task * set_size + group * LOW, LOW)
        ids_row = jnp.sum(jnp.where(own, ids_all[pl.ds(base, LOW), :], 0.0), axis=0, keepdims=True)
        match = (member == ids_row).astype(jnp.float32)
        spread_match = jnp.concatenate(
            [jnp.where(owner_wide == low, match, 0.0).astype(half) for low in range(LOW)], axis=0
        )
        stacked = jnp.concatenate(
            [
                cols[pl.ds(pl.multiple_of(place_ref[task, group * LOW + low] * links, links), links), :]
                for low in range(LOW)
            ],
            axis=0,
        )
        product[...] = nn(spread_match, stacked)
        for low in range(LOW):
            row = low * set_size + group * LOW + low
            product[pl.ds(row, 1), :] = onsite_all[pl.ds(base + low, 1), :]
        ordered = nn(product[...].astype(half), reorder)
        for high in range(area // LANES):
            tiles = [
                ordered[low * set_size : (low + 1) * set_size, high * LANES : (high + 1) * LANES] for low in range(LOW)
            ]
            for step in (1, 2, 4):
                keep = (lane & step) == 0
                for low in range(LOW):
                    if low & step:
                        continue
                    first, second = tiles[low], tiles[low | step]
                    tiles[low] = jnp.where(keep, first, pltpu.roll(second, step, 1))
                    tiles[low | step] = jnp.where(keep, pltpu.roll(first, LANES - step, 1), second)
            for low in range(LOW):
                for upper in range(set_size // LOW):
                    matrix[
                        pl.ds(upper * LANES + (high * LOW + low) * LOW, LOW), pl.ds(group * LANES, LANES)
                    ] = tiles[low][upper * LOW : (upper + 1) * LOW]

    on_diagonal = iota((order, order), 0) == iota((order, order), 1)
    identity = on_diagonal.astype(jnp.float32)
    mirrored = nt(identity.astype(half), matrix[...].astype(half))
    whole = 0.5 * (matrix[...] + mirrored) - shift_ref[task] * identity
    bound = jnp.max(jnp.sum(jnp.abs(whole), axis=0)) + 1e-06
    iterate = (whole / bound).astype(half)
    for _ in range(ITERS - 1):
        factor = (1.5 * identity - 0.5 * nn(iterate, iterate)).astype(half)
        iterate = nn(iterate, factor).astype(half)
    left = identity[:, :CENTRAL]
    factor = (1.5 * left - 0.5 * nn(iterate, iterate[:, :CENTRAL])).astype(half)
    turned = (0.5 * (left - nn(iterate, factor))).astype(half)

    source, target = iota((LANES, LANES), 0), iota((LANES, LANES), 1)
    back = (source == (target % BS) * LOW + target // BS).astype(jnp.float32).astype(half)
    front = (target == (source % BS) * LOW + source // BS).astype(jnp.float32).astype(half)
    mid = nn(turned, back).astype(half)
    tall = nt(front, turned).astype(half)
    wide = []
    for upper in range(order // LANES):
        part = pl.ds(upper * LANES, LANES)
        density_ref[0, part, :] = nn(front, mid[upper * LANES : (upper + 1) * LANES]).astype(half)
        wide.append(nn(tall[:, upper * LANES : (upper + 1) * LANES], back).astype(half))
    weights = nn(jnp.concatenate(wide, axis=1), basis_ref[0])
    values = jnp.sum(weights * basis_ref[0, :CENTRAL, :].astype(jnp.float32), axis=0, keepdims=True)
    rows = values.shape[1] // LANES
    box_ref[0] = jnp.concatenate(
        [values[:, row * LANES : (row + 1) * LANES] for row in range(rows)], axis=0
    ).astype(half)


def slab_kernel(start_ref, row_ref, col_ref, boxes_ref, slab_ref, work):
    planes = slab_ref.shape[0]
    work[...] = jnp.zeros_like(work)
    per_row = LANES // BOX_COLS
    lane, within = iota((per_row, LANES), 1), iota((per_row, LANES), 0)
    tiles_per_plane = BOX_ROWS // per_row

    def add(index, carry):
        first = start_ref[index]

        @pl.when(jnp.logical_and(first > -BOXP, first < planes))
        def _():
            row, col = row_ref[index], col_ref[index]
            box = pltpu.roll(boxes_ref[index].astype(jnp.float32), col, 1)
            inside = jnp.logical_and(lane >= col, lane < col + BOX_COLS)
            for plane in range(BOXP):
                for part in range(tiles_per_plane):
                    at = plane * tiles_per_plane + part
                    moved = jnp.broadcast_to(box[at : at + 1, :], (per_row, LANES))
                    step = 1
                    while step < per_row:
                        turned = pltpu.roll(moved, LANES - step * BOX_COLS, 1)
                        moved = jnp.where(within & step == 0, moved, turned)
                        step *= 2
                    moved = jnp.where(inside, moved, 0.0)
                    where = pl.ds(row + part * per_row, per_row)
                    work[first + BOXP - 1 + plane, where, :] += moved
        return carry

    lax.fori_loop(0, start_ref.shape[0], add, 0)
    slab_ref[...] = work[pl.ds(BOXP - 1, planes)]


def on_device(
    column_blocks,
    onsite,
    neighbor_ids,
    task_atoms,
    chem_shift,
    basis_values,
    box_start,
    box_row,
    box_col,
):
    half = jnp.bfloat16
    holders = lax.axis_size("atoms")
    atoms_here, links, area = column_blocks.shape
    tasks, set_size = task_atoms.shape
    order, points = basis_values.shape[1:]
    corners = gather_everywhere(jnp.stack([box_start, box_row, box_col], axis=1))
    idents = jnp.concatenate([neighbor_ids % 256, neighbor_ids // 256], axis=1).astype(half)
    idents = jnp.pad(idents, ((0, 0), (0, area - 2 * links)))
    packed = jnp.concatenate([column_blocks.reshape(atoms_here * links, area), onsite, idents], axis=0)
    pieces, slot = gather_columns(packed, holders)
    place = slot(task_atoms // atoms_here) * atoms_here + task_atoms % atoms_here
    everything = pl.BlockSpec(memory_space=pl.ANY)
    scalars = pl.BlockSpec(memory_space=pltpu.SMEM)
    density, boxes = pl.pallas_call(
        functools.partial(density_kernel, holders, atoms_here, links),
        grid=(tasks,),
        in_specs=[
            scalars,
            scalars,
            pl.BlockSpec((tasks * set_size, 1), lambda t: (0, 0)),
            pl.BlockSpec((1, set_size, 1), lambda t: (t, 0, 0)),
            pl.BlockSpec((1, order, points), lambda t: (t, 0, 0)),
        ]
        + [everything] * holders,
        out_specs=[
            pl.BlockSpec((1, order, CENTRAL), lambda t: (t, 0, 0)),
            pl.BlockSpec((1, points // LANES, LANES), lambda t: (t, 0, 0)),
        ],
        out_shape=[
            jax.ShapeDtypeStruct((tasks, order, CENTRAL), half),
            jax.ShapeDtypeStruct((tasks, points // LANES, LANES), half),
        ],
        scratch_shapes=[
            pltpu.VMEM((holders * atoms_here * links, area), half),
            pltpu.VMEM((holders * atoms_here, area), half),
            pltpu.VMEM((holders * atoms_here, area), half),
            pltpu.VMEM((tasks * set_size, LOW * links), jnp.float32),
            pltpu.VMEM((tasks * set_size, area), jnp.float32),
            pltpu.VMEM((LOW * set_size, area), jnp.float32),
            pltpu.VMEM((order, order), jnp.float32),
            pltpu.SemaphoreType.DMA((3, holders)),
        ],
        compiler_params=pltpu.CompilerParams(vmem_limit_bytes=52 * 1024 * 1024),
    )(
        place,
        chem_shift,
        place.reshape(-1, 1),
        task_atoms.astype(jnp.float32)[:, :, None],
        basis_values,
        *pieces,
    )
    all_boxes = gather_everywhere(boxes)
    starts = corners[:, 0] - lax.axis_index("grid") * PL_SLAB
    slab = pl.pallas_call(
        slab_kernel,
        in_specs=[scalars, scalars, scalars, pl.BlockSpec(memory_space=pltpu.VMEM)],
        out_specs=pl.BlockSpec(memory_space=pltpu.VMEM),
        out_shape=jax.ShapeDtypeStruct((PL_SLAB, GRID_ROWS, GRID_COLS), jnp.float32),
        scratch_shapes=[pltpu.VMEM((PL_SLAB + 2 * (BOXP - 1), GRID_ROWS, GRID_COLS), jnp.float32)],
        compiler_params=pltpu.CompilerParams(vmem_limit_bytes=32 * 1024 * 1024),
    )(starts, corners[:, 1], corners[:, 2], all_boxes)
    return density, slab


def solution(mesh):
    placed = (
        P("atoms", None, None),
        P("atoms", None),
        P("atoms", None),
        P(("atoms", "grid"), None),
        P(("atoms", "grid")),
        P(("atoms", "grid"), None, None),
        P(("atoms", "grid")),
        P(("atoms", "grid")),
        P(("atoms", "grid")),
    )
    return jax.shard_map(
        on_device,
        mesh=mesh,
        in_specs=placed,
        out_specs=(P(("atoms", "grid"), None, None), P("grid", None, None)),
        check_vma=False,
    )
```

```python
import functools

import jax
import jax.numpy as jnp
from jax import lax
from jax.experimental import pallas as pl
from jax.experimental.pallas import tpu as pltpu
from jax.sharding import PartitionSpec as P

BS = 16
ITERS = 3
BOXP = 4
BOX_ROWS = 16
BOX_COLS = 16
GRID_ROWS = 32
GRID_COLS = 128
PL_SLAB = 64
CENTRAL = 128

LOW = 8
LANES = 128
BATCH = 4
STAGGER = 1


def doubled(value, axis, size, pairs):
    for step in pairs:
        other = lax.ppermute(value, axis, [(i, i ^ step) for i in range(size)])
        value = jnp.concatenate([value, other], axis=0)
    return value


def power_of_two(size):
    return size & (size - 1) == 0


def gather_everywhere(value):
    for axis in ("grid", "atoms"):
        size = lax.axis_size(axis)
        if power_of_two(size):
            steps = [1 << bit for bit in range(size.bit_length() - 1)][::-1]
            value = doubled(value, axis, size, steps)
        else:
            value = lax.all_gather(value, axis, axis=0, tiled=True)
    return value


def gather_columns(packed, holders):
    if holders < 2 or not power_of_two(holders):
        whole = lax.all_gather(packed, "atoms", axis=0)
        return [whole[i] for i in range(holders)], lambda holder: holder
    stages = holders.bit_length() - 2
    half = holders // 2

    def bit_of(device, stage):
        return 2 << (stages - 1 - stage if device & 1 else stage)

    pieces = [packed]
    for stage in range(stages):
        pairs = [(i, i ^ bit_of(i, stage)) for i in range(holders)]
        pieces = pieces + [lax.ppermute(piece, "atoms", pairs) for piece in pieces]
    swap = [(i, i ^ 1) for i in range(holders)]
    pieces = pieces + [lax.ppermute(piece, "atoms", swap) for piece in pieces]

    def slot(holder):
        apart = holder ^ lax.axis_index("atoms")
        plain = apart >> 1
        turned = sum((((plain >> bit) & 1) << (stages - 1 - bit) for bit in range(stages)), 0 * plain)
        return (apart & 1) * half + jnp.where(holder & 1 == 1, turned, plain)

    return pieces, slot


def iota(shape, axis):
    return lax.broadcasted_iota(jnp.int32, shape, axis)


def nn(left, right):
    return jnp.dot(left, right, preferred_element_type=jnp.float32)


def nt(left, right):
    return lax.dot_general(left, right, (((1,), (1,)), ((), ())), preferred_element_type=jnp.float32)


def plus_diagonal(value, scale, amount):
    here = iota((LANES, LANES), 0) == iota((LANES, LANES), 1)
    diagonal = jnp.where(here, amount, 0.0)
    rows, columns = value.shape
    out = []
    for row in range(0, rows, LANES):
        part = scale * value[row : row + LANES]
        if row < columns:
            pieces = [part[:, :row], part[:, row : row + LANES] + diagonal, part[:, row + LANES :]]
            part = jnp.concatenate([piece for piece in pieces if piece.shape[1]], axis=1)
        out.append(part)
    return jnp.concatenate(out, axis=0)


def density_kernel(
    holders,
    atoms_here,
    links,
    place_ref,
    shift_ref,
    start_ref,
    row_ref,
    col_ref,
    slot_col_ref,
    member_col_ref,
    basis_hbm,
    *rest,
):
    pieces = rest[:holders]
    (
        density_hbm,
        box_ref,
        cols,
        onsites,
        idents,
        basis,
        density,
        ids_all,
        onsite_all,
        product,
        matrix,
        sems,
        basis_sems,
        density_sems,
    ) = rest[holders:]
    half = jnp.bfloat16
    tasks, set_size = member_col_ref.shape[:2]
    order = set_size * BS
    area = BS * BS
    block_rows = atoms_here * links
    groups = set_size // LOW

    copies = []
    for number, piece in enumerate(pieces):
        spots = (
            (cols, 0, block_rows),
            (onsites, block_rows, atoms_here),
            (idents, block_rows + atoms_here, atoms_here),
        )
        for kind, (target, first, count) in enumerate(spots):
            copies.append(
                pltpu.make_async_copy(
                    piece.at[pl.ds(first, count)], target.at[pl.ds(number * count, count)], sems.at[kind, number]
                )
            )
    loads = [pltpu.make_async_copy(basis_hbm.at[t], basis.at[t], basis_sems.at[t]) for t in range(tasks)]
    stores = [pltpu.make_async_copy(density.at[t], density_hbm.at[t], density_sems.at[t]) for t in range(tasks)]
    for copy in copies:
        copy.start()
    for copy in copies:
        copy.wait()
    for load in loads:
        load.start()
    count = tasks * set_size
    chosen = (slot_col_ref[...] == iota((count, holders * atoms_here), 1)).astype(jnp.float32).astype(half)
    onsite_all[...] = nn(chosen, onsites[...])
    raw = nn(chosen, idents[...]).astype(half)
    source, target = iota((area, LOW * links), 0), iota((area, LOW * links), 1) % links
    spread = jnp.where(source == target, 1.0, jnp.where(source == links + target, 256.0, 0.0)).astype(half)
    ids_all[...] = nn(raw, spread)

    source, target = iota((area, area), 0), iota((area, area), 1)
    wanted = ((target // LANES) * LOW + target % LOW) * BS + (target % LANES) // LOW
    reorder = (source == wanted).astype(jnp.float32).astype(half)
    identity = (iota((order, order), 0) == iota((order, order), 1)).astype(jnp.float32).astype(half)
    source, target = iota((LANES, LANES), 0), iota((LANES, LANES), 1)
    back = (source == (target % BS) * LOW + target // BS).astype(jnp.float32).astype(half)
    front = (target == (source % BS) * LOW + source // BS).astype(jnp.float32).astype(half)

    lane_owner = iota((LOW, LOW * links), 1) // links
    own = lane_owner == iota((LOW, LOW * links), 0)
    owner_wide = iota((set_size, LOW * links), 1) // links
    lane = iota((set_size, LANES), 1)
    boxes = {}

    def assemble(task, group):
        base = task * set_size + group * LOW
        ids_row = jnp.sum(jnp.where(own, ids_all[pl.ds(base, LOW), :], 0.0), axis=0, keepdims=True)
        match = (member_col_ref[task] == ids_row).astype(jnp.float32)
        spread_match = jnp.concatenate(
            [jnp.where(owner_wide == low, match, 0.0).astype(half) for low in range(LOW)], axis=0
        )
        stacked = jnp.concatenate(
            [
                cols[pl.ds(pl.multiple_of(place_ref[task, group * LOW + low] * links, links), links), :]
                for low in range(LOW)
            ],
            axis=0,
        )
        spot = product.at[task, group % 2]
        spot[...] = nn(spread_match, stacked)
        for low in range(LOW):
            row = low * set_size + group * LOW + low
            spot[pl.ds(row, 1), :] = onsite_all[pl.ds(base + low, 1), :]
        ordered = nn(spot[...].astype(half), reorder)
        for high in range(area // LANES):
            tiles = [
                ordered[low * set_size : (low + 1) * set_size, high * LANES : (high + 1) * LANES] for low in range(LOW)
            ]
            for step in (1, 2, 4):
                keep = (lane & step) == 0
                for low in range(LOW):
                    if low & step:
                        continue
                    first, second = tiles[low], tiles[low | step]
                    tiles[low] = jnp.where(keep, first, pltpu.roll(second, step, 1))
                    tiles[low | step] = jnp.where(keep, pltpu.roll(first, LANES - step, 1), second)
            for low in range(LOW):
                for upper in range(set_size // LOW):
                    matrix[
                        task,
                        pl.ds(upper * LANES + (high * LOW + low) * LOW, LOW),
                        pl.ds(group * LANES, LANES),
                    ] = tiles[low][upper * LOW : (upper + 1) * LOW]

    def steps_of(task):
        for group in range(groups):
            assemble(task, group)
            yield
        mirrored = nt(identity, matrix[task].astype(half))
        yield
        whole = plus_diagonal(matrix[task] + mirrored, 0.5, -shift_ref[task])
        bound = jnp.max(jnp.sum(jnp.abs(whole), axis=0, keepdims=True), axis=1, keepdims=True) + 1e-06
        iterate = (whole * (1.0 / bound)).astype(half)
        yield
        for _ in range(ITERS - 1):
            factor = plus_diagonal(nn(iterate, iterate), -0.5, 1.5).astype(half)
            yield
            iterate = nn(iterate, factor).astype(half)
            yield
        factor = plus_diagonal(nn(iterate, iterate[:, :CENTRAL]), -0.5, 1.5).astype(half)
        yield
        turned = plus_diagonal(nn(iterate, factor), -0.5, 0.5).astype(half)
        yield
        mid = nn(turned, back).astype(half)
        tall = nt(front, turned).astype(half)
        wide = []
        for upper in range(order // LANES):
            part = slice(upper * LANES, (upper + 1) * LANES)
            density[task, part, :] = nn(front, mid[part]).astype(half)
            wide.append(nn(tall[:, part], back).astype(half))
        stores[task].start()
        yield
        loads[task].wait()
        weights = nn(jnp.concatenate(wide, axis=1), basis[task])
        values = jnp.sum(weights * basis[task, :CENTRAL, :].astype(jnp.float32), axis=0, keepdims=True)
        rows = values.shape[1] // LANES
        box = jnp.concatenate([values[:, row * LANES : (row + 1) * LANES] for row in range(rows)], axis=0)
        boxes[task] = pltpu.roll(box, col_ref[task], 1)
        yield

    running = []
    waiting = [steps_of(task) for task in range(tasks)]
    tick = 0
    while running or waiting:
        if waiting and tick % STAGGER == 0:
            running.append(waiting.pop(0))
        for steps in list(running):
            if next(steps, running) is running:
                running.remove(steps)
        tick += 1

    lane = iota((1, LANES), 1)
    corner = jnp.zeros((1, LANES), jnp.float32)
    for task in range(tasks):
        numbers = (start_ref[task] // PL_SLAB, start_ref[task] % PL_SLAB, row_ref[task], col_ref[task])
        for place, number in enumerate(numbers):
            corner = jnp.where(lane == task * len(numbers) + place, number.astype(jnp.float32), corner)
    box_rows = [boxes[task] for task in range(tasks)]
    rest_rows = box_ref.shape[0] - sum(box.shape[0] for box in box_rows) - 1
    box_ref[...] = jnp.concatenate(
        box_rows + [corner, jnp.zeros((rest_rows, LANES), jnp.float32)], axis=0
    ).astype(half)
    for store in stores:
        store.wait()


def slab_kernel(tasks, slab_number_ref, boxes_ref, slab_ref, work, wide, unfolded, corner_vmem, corners, chosen, sem):
    planes = slab_ref.shape[0]
    devices = boxes_ref.shape[0]
    per_row = LANES // BOX_COLS
    box_rows = BOXP * BOX_ROWS // per_row
    corner_at = tasks * box_rows
    numbers = boxes_ref[:, corner_at : corner_at + LOW, :].astype(jnp.float32)[:, 0, :].astype(jnp.int32)
    first = (pltpu.roll(numbers, 1, 1) - slab_number_ref[0]) * planes + numbers
    corner_vmem[...] = jnp.where(iota(numbers.shape, 1) % 4 == 1, first, numbers)
    copy = pltpu.make_async_copy(corner_vmem, corners, sem)
    copy.start()
    work[...] = jnp.zeros_like(work)
    wide[...] = boxes_ref[:, :corner_at, :].astype(jnp.float32).reshape(devices * tasks, box_rows, LANES)
    lane = iota((per_row, LANES), 1)
    copy.wait()

    def look(device, count):
        for task in range(tasks):
            first = corners[device, 4 * task + 1]
            chosen[count] = device * tasks + task
            count += jnp.logical_and(first > -BOXP, first < planes).astype(jnp.int32)
        return count

    count = lax.fori_loop(0, devices, look, 0)
    for extra in range(BATCH):
        chosen[count + extra] = -1

    def add(turn, carry):
        places = []
        for part in range(BATCH):
            index = chosen[turn * BATCH + part]
            box = jnp.maximum(index, 0)
            device, task = box // tasks, box % tasks
            first = jnp.where(index < 0, planes + BOXP - 1, corners[device, 4 * task + 1])
            row, col = corners[device, 4 * task + 2], corners[device, 4 * task + 3]
            places.append((first + BOXP - 1, row))
            inside = jnp.logical_and(lane >= col, lane < col + BOX_COLS)
            rows = wide[box]
            for within in range(per_row):
                turned = rows if within == 0 else pltpu.roll(rows, LANES - within * BOX_COLS, 1)
                unfolded[part, pl.ds(within * box_rows, box_rows), :] = jnp.where(inside, turned, 0.0)
        for part, (plane, row) in enumerate(places):
            for at in range(box_rows):
                tile = unfolded[part, pl.ds(at, per_row, stride=box_rows), :]
                where = pl.ds(row + at % (BOX_ROWS // per_row) * per_row, per_row)
                work[plane + at // (BOX_ROWS // per_row), where, :] += tile
        return carry

    lax.fori_loop(0, (count + BATCH - 1) // BATCH, add, 0)
    slab_ref[...] = work[pl.ds(BOXP - 1, planes)]


def on_device(
    column_blocks,
    onsite,
    neighbor_ids,
    task_atoms,
    chem_shift,
    basis_values,
    box_start,
    box_row,
    box_col,
):
    half = jnp.bfloat16
    holders = lax.axis_size("atoms")
    atoms_here, links, area = column_blocks.shape
    tasks, set_size = task_atoms.shape
    order, points = basis_values.shape[1:]
    idents = jnp.concatenate([neighbor_ids % 256, neighbor_ids // 256], axis=1).astype(half)
    idents = jnp.pad(idents, ((0, 0), (0, area - 2 * links)))
    packed = jnp.concatenate([column_blocks.reshape(atoms_here * links, area), onsite, idents], axis=0)
    pieces, slot = gather_columns(packed, holders)
    place = slot(task_atoms // atoms_here) * atoms_here + task_atoms % atoms_here
    everything = pl.BlockSpec(memory_space=pl.ANY)
    scalars = pl.BlockSpec(memory_space=pltpu.SMEM)
    vectors = pl.BlockSpec(memory_space=pltpu.VMEM)
    box_rows = (tasks * points // LANES + 1 + 15) // 16 * 16
    column_bytes = packed.size * holders * 2
    density, boxes = pl.pallas_call(
        functools.partial(density_kernel, holders, atoms_here, links),
        in_specs=[scalars] * 5 + [vectors] * 2 + [pl.BlockSpec(memory_space=pltpu.HBM)] + [everything] * holders,
        out_specs=[everything, vectors],
        out_shape=[
            jax.ShapeDtypeStruct((tasks, order, CENTRAL), half),
            jax.ShapeDtypeStruct((box_rows, LANES), half),
        ],
        scratch_shapes=[
            pltpu.VMEM((holders * atoms_here * links, area), half),
            pltpu.VMEM((holders * atoms_here, area), half),
            pltpu.VMEM((holders * atoms_here, area), half),
            pltpu.VMEM((tasks, order, points), half),
            pltpu.VMEM((tasks, order, CENTRAL), half),
            pltpu.VMEM((tasks * set_size, LOW * links), jnp.float32),
            pltpu.VMEM((tasks * set_size, area), jnp.float32),
            pltpu.VMEM((tasks, 2, LOW * set_size, area), jnp.float32),
            pltpu.VMEM((tasks, order, order), jnp.float32),
            pltpu.SemaphoreType.DMA((3, holders)),
            pltpu.SemaphoreType.DMA((tasks,)),
            pltpu.SemaphoreType.DMA((tasks,)),
        ],
        compiler_params=pltpu.CompilerParams(vmem_limit_bytes=48 * 1024 * 1024),
    )(
        place,
        chem_shift,
        box_start,
        box_row,
        box_col,
        place.reshape(-1, 1),
        task_atoms.astype(jnp.float32)[:, :, None],
        basis_values,
        *pieces,
    )
    all_boxes = gather_everywhere(boxes[None])
    slab_number = lax.axis_index("grid").astype(jnp.int32).reshape(1)
    slab = pl.pallas_call(
        functools.partial(slab_kernel, tasks),
        in_specs=[scalars, vectors],
        out_specs=vectors,
        out_shape=jax.ShapeDtypeStruct((PL_SLAB, GRID_ROWS, GRID_COLS), jnp.float32),
        scratch_shapes=[
            pltpu.VMEM((PL_SLAB + 3 * BOXP, GRID_ROWS, GRID_COLS), jnp.float32),
            pltpu.VMEM((all_boxes.shape[0] * tasks, points // LANES, LANES), jnp.float32),
            pltpu.VMEM((BATCH, points // BOX_COLS, LANES), jnp.float32),
            pltpu.VMEM((all_boxes.shape[0], LANES), jnp.int32),
            pltpu.SMEM((all_boxes.shape[0], LANES), jnp.int32),
            pltpu.SMEM((all_boxes.shape[0] * tasks + BATCH,), jnp.int32),
            pltpu.SemaphoreType.DMA,
        ],
        compiler_params=pltpu.CompilerParams(vmem_limit_bytes=32 * 1024 * 1024),
    )(slab_number, all_boxes)
    return density, slab


def solution(mesh):
    placed = (
        P("atoms", None, None),
        P("atoms", None),
        P("atoms", None),
        P(("atoms", "grid"), None),
        P(("atoms", "grid")),
        P(("atoms", "grid"), None, None),
        P(("atoms", "grid")),
        P(("atoms", "grid")),
        P(("atoms", "grid")),
    )
    return jax.shard_map(
        on_device,
        mesh=mesh,
        in_specs=placed,
        out_specs=(P(("atoms", "grid"), None, None), P("grid", None, None)),
        check_vma=False,
    )
```

```python
import functools

import jax
import jax.numpy as jnp
from jax import lax
from jax.experimental import pallas as pl
from jax.experimental.pallas import tpu as pltpu
from jax.sharding import PartitionSpec as P

BS = 16
ITERS = 3
BOXP = 4
BOX_ROWS = 16
BOX_COLS = 16
GRID_ROWS = 32
GRID_COLS = 128
PL_SLAB = 64
CENTRAL = 128

LOW = 8
LANES = 128
BATCH = 4
STAGGER = 1


def power_of_two(size):
    return size & (size - 1) == 0


def gather_everywhere(value):
    for axis in ("grid", "atoms"):
        size = lax.axis_size(axis)
        if not power_of_two(size):
            value = lax.all_gather(value, axis, axis=0, tiled=True)
            continue
        steps = [1 << bit for bit in range(size.bit_length() - 1)][::-1]
        for stage, step in enumerate(steps):
            pairs = [(i, i ^ step) for i in range(size)]
            if axis == "atoms" and step > 1:
                pairs = [(i, i ^ (steps[len(steps) - 2 - stage] if i & 1 else step)) for i in range(size)]
            value = jnp.concatenate([value, lax.ppermute(value, axis, pairs)], axis=0)
    return value


def split(number, size):
    if power_of_two(size):
        return number >> (size.bit_length() - 1), number & (size - 1)
    return number // size, number % size


def slot_of(holder, holders):
    if holders < 2 or not power_of_two(holders):
        return holder
    stages = holders.bit_length() - 2
    apart = holder ^ lax.axis_index("atoms")
    plain = apart >> 1
    turned = sum((((plain >> bit) & 1) << (stages - 1 - bit) for bit in range(stages)), 0 * plain)
    return (apart & 1) * (holders // 2) + jnp.where(holder & 1 == 1, turned, plain)


def gather_columns(blocks, side, holders):
    if holders < 2 or not power_of_two(holders):
        gathered = [lax.all_gather(part, "atoms", axis=0) for part in (blocks, side())]
        return [[whole[i] for i in range(holders)] for whole in gathered]
    stages = holders.bit_length() - 2

    def bit_of(device, stage):
        return 2 << (stages - 1 - stage if device & 1 else stage)

    pairs = [[(i, i ^ bit_of(i, stage)) for i in range(holders)] for stage in range(stages)]
    swap = [(i, i ^ 1) for i in range(holders)]

    def send(part):
        return [lax.ppermute(part, "atoms", pair) for pair in pairs]

    def forward(part, firsts):
        have = [part]
        for first, pair in zip(firsts, pairs):
            have = have + [first] + [lax.ppermute(piece, "atoms", pair) for piece in have[1:]]
        return have

    firsts = send(blocks)
    beside = lax.ppermute(blocks, "atoms", swap)
    beside, wanted = lax.optimization_barrier((beside, side()))
    side_firsts = send(wanted)
    if stages:
        firsts[0], side_firsts = lax.optimization_barrier((firsts[0], side_firsts))
    have, side_have = forward(blocks, firsts), forward(wanted, side_firsts)
    swapped = [beside] + [lax.ppermute(piece, "atoms", swap) for piece in have[1:-1]]
    side_swapped = [lax.ppermute(piece, "atoms", swap) for piece in side_have[:-1]]
    mine = jnp.concatenate([blocks, wanted[:, : blocks.shape[1]]], axis=0)
    have[-1], side_have[-1], swapped, side_swapped, mine = lax.optimization_barrier(
        (have[-1], side_have[-1], swapped, side_swapped, mine)
    )
    if stages:
        swapped.append(lax.ppermute(have[-1], "atoms", swap))
    side_swapped.append(lax.ppermute(side_have[-1], "atoms", swap))
    return [[mine] + have[1:] + swapped, side_have + side_swapped]


def iota(shape, axis):
    return lax.broadcasted_iota(jnp.int32, shape, axis)


def nn(left, right):
    return jnp.dot(left, right, preferred_element_type=jnp.float32)


def nt(left, right):
    return lax.dot_general(left, right, (((1,), (1,)), ((), ())), preferred_element_type=jnp.float32)


def plus_diagonal(value, scale, amount):
    here = iota((LANES, LANES), 0) == iota((LANES, LANES), 1)
    diagonal = jnp.where(here, amount, 0.0)
    rows, columns = value.shape
    out = []
    for row in range(0, rows, LANES):
        part = scale * value[row : row + LANES]
        if row < columns:
            pieces = [part[:, :row], part[:, row : row + LANES] + diagonal, part[:, row + LANES :]]
            part = jnp.concatenate([piece for piece in pieces if piece.shape[1]], axis=1)
        out.append(part)
    return jnp.concatenate(out, axis=0)


def density_kernel(
    holders,
    atoms_here,
    links,
    shift_ref,
    start_ref,
    row_ref,
    col_ref,
    members_ref,
    basis_hbm,
    *rest,
):
    pieces, extras = rest[:holders], rest[holders : 2 * holders]
    (
        density_hbm,
        box_ref,
        cols,
        sides,
        basis,
        density,
        ids_all,
        onsite_all,
        product,
        matrix,
        place_vmem,
        place_ref,
        place_sem,
        sems,
        basis_sems,
        density_sems,
    ) = rest[2 * holders :]
    half = jnp.bfloat16
    tasks, set_size = members_ref.shape
    order = set_size * BS
    area = BS * BS
    block_rows = atoms_here * links
    groups = set_size // LOW

    copies = []
    for kind, (parts, whole, count) in enumerate(((extras, sides, atoms_here), (pieces, cols, block_rows))):
        for number, part in enumerate(parts):
            target = whole.at[pl.ds(number * count, count)]
            copies.append(pltpu.make_async_copy(part.at[pl.ds(0, count)], target, sems.at[kind, number]))
    loads = [pltpu.make_async_copy(basis_hbm.at[t], basis.at[t], basis_sems.at[t]) for t in range(tasks)]
    stores = [pltpu.make_async_copy(density.at[t], density_hbm.at[t], density_sems.at[t]) for t in range(tasks)]
    for copy in copies:
        copy.start()
    held_by, held_at = split(members_ref[...], atoms_here)
    slots = slot_of(held_by, holders) * atoms_here + held_at
    place_vmem[...] = slots
    place_copy = pltpu.make_async_copy(place_vmem, place_ref, place_sem)
    place_copy.start()
    for copy in copies[:holders]:
        copy.wait()
    atoms = iota((set_size, holders * atoms_here), 1).astype(jnp.float32)
    diagonal = iota((set_size, set_size), 0) == iota((set_size, set_size), 1)

    def column(rows, task):
        row = rows[task : task + 1].astype(jnp.float32)
        return jnp.sum(jnp.where(diagonal, row, 0.0), axis=1, keepdims=True)

    members = [column(members_ref[...], task) for task in range(tasks)]
    chosen = jnp.concatenate(
        [(column(slots, task) == atoms).astype(jnp.float32) for task in range(tasks)], axis=0
    ).astype(half)
    onsite_all[...] = nn(chosen, sides[:, :area])
    raw = nn(chosen, sides[:, area:]).astype(half)
    source, target = iota((area, LOW * links), 0), iota((area, LOW * links), 1) % links
    spread = jnp.where(source == target, 1.0, jnp.where(source == links + target, 256.0, 0.0)).astype(half)
    ids_all[...] = nn(raw, spread)
    place_copy.wait()
    for copy in copies[holders:]:
        copy.wait()
    for load in loads:
        load.start()

    source, target = iota((area, area), 0), iota((area, area), 1)
    wanted = ((target // LANES) * LOW + target % LOW) * BS + (target % LANES) // LOW
    reorder = (source == wanted).astype(jnp.float32).astype(half)
    identity = (iota((order, order), 0) == iota((order, order), 1)).astype(jnp.float32).astype(half)
    source, target = iota((LANES, LANES), 0), iota((LANES, LANES), 1)
    back = (source == (target % BS) * LOW + target // BS).astype(jnp.float32).astype(half)
    front = (target == (source % BS) * LOW + source // BS).astype(jnp.float32).astype(half)

    lane_owner = iota((LOW, LOW * links), 1) // links
    own = lane_owner == iota((LOW, LOW * links), 0)
    owner_wide = iota((set_size, LOW * links), 1) // links
    lane = iota((set_size, LANES), 1)
    boxes = {}

    def assemble(task, group):
        base = task * set_size + group * LOW
        ids_row = jnp.sum(jnp.where(own, ids_all[pl.ds(base, LOW), :], 0.0), axis=0, keepdims=True)
        match = (members[task] == ids_row).astype(jnp.float32)
        spread_match = jnp.concatenate(
            [jnp.where(owner_wide == low, match, 0.0).astype(half) for low in range(LOW)], axis=0
        )
        stacked = jnp.concatenate(
            [
                cols[pl.ds(pl.multiple_of(place_ref[task, group * LOW + low] * links, links), links), :]
                for low in range(LOW)
            ],
            axis=0,
        )
        spot = product.at[task, group % 2]
        spot[...] = nn(spread_match, stacked)
        for low in range(LOW):
            row = low * set_size + group * LOW + low
            spot[pl.ds(row, 1), :] = onsite_all[pl.ds(base + low, 1), :]
        ordered = nn(spot[...].astype(half), reorder)
        for high in range(area // LANES):
            tiles = [
                ordered[low * set_size : (low + 1) * set_size, high * LANES : (high + 1) * LANES] for low in range(LOW)
            ]
            for step in (1, 2, 4):
                keep = (lane & step) == 0
                for low in range(LOW):
                    if low & step:
                        continue
                    first, second = tiles[low], tiles[low | step]
                    tiles[low] = jnp.where(keep, first, pltpu.roll(second, step, 1))
                    tiles[low | step] = jnp.where(keep, pltpu.roll(first, LANES - step, 1), second)
            for low in range(LOW):
                for upper in range(set_size // LOW):
                    matrix[
                        task,
                        pl.ds(upper * LANES + (high * LOW + low) * LOW, LOW),
                        pl.ds(group * LANES, LANES),
                    ] = tiles[low][upper * LOW : (upper + 1) * LOW]

    def steps_of(task):
        for group in range(groups):
            assemble(task, group)
            yield
        mirrored = nt(identity, matrix[task].astype(half))
        yield
        whole = plus_diagonal(matrix[task] + mirrored, 0.5, -shift_ref[task])
        bound = jnp.max(jnp.sum(jnp.abs(whole), axis=0, keepdims=True), axis=1, keepdims=True) + 1e-06
        iterate = (whole * (1.0 / bound)).astype(half)
        yield
        for _ in range(ITERS - 1):
            factor = plus_diagonal(nn(iterate, iterate), -0.5, 1.5).astype(half)
            yield
            iterate = nn(iterate, factor).astype(half)
            yield
        factor = plus_diagonal(nn(iterate, iterate[:, :CENTRAL]), -0.5, 1.5).astype(half)
        yield
        turned = plus_diagonal(nn(iterate, factor), -0.5, 0.5).astype(half)
        yield
        mid = nn(turned, back).astype(half)
        tall = nt(front, turned).astype(half)
        wide = []
        for upper in range(order // LANES):
            part = slice(upper * LANES, (upper + 1) * LANES)
            density[task, part, :] = nn(front, mid[part]).astype(half)
            wide.append(nn(tall[:, part], back).astype(half))
        stores[task].start()
        yield
        loads[task].wait()
        weights = nn(jnp.concatenate(wide, axis=1), basis[task])
        values = jnp.sum(weights * basis[task, :CENTRAL, :].astype(jnp.float32), axis=0, keepdims=True)
        rows = values.shape[1] // LANES
        box = jnp.concatenate([values[:, row * LANES : (row + 1) * LANES] for row in range(rows)], axis=0)
        boxes[task] = pltpu.roll(box, col_ref[task], 1)
        yield

    running = []
    waiting = [steps_of(task) for task in range(tasks)]
    tick = 0
    while running or waiting:
        if waiting and tick % STAGGER == 0:
            running.append(waiting.pop(0))
        for steps in list(running):
            if next(steps, running) is running:
                running.remove(steps)
        tick += 1

    lane = iota((1, LANES), 1)
    corner = jnp.zeros((1, LANES), jnp.float32)
    for task in range(tasks):
        numbers = (start_ref[task] // PL_SLAB, start_ref[task] % PL_SLAB, row_ref[task], col_ref[task])
        for place, number in enumerate(numbers):
            corner = jnp.where(lane == task * len(numbers) + place, number.astype(jnp.float32), corner)
    box_rows = [boxes[task] for task in range(tasks)]
    rest_rows = box_ref.shape[0] - sum(box.shape[0] for box in box_rows) - 1
    box_ref[...] = jnp.concatenate(
        box_rows + [corner, jnp.zeros((rest_rows, LANES), jnp.float32)], axis=0
    ).astype(half)
    for store in stores:
        store.wait()


def slab_kernel(tasks, slab_number_ref, boxes_ref, slab_ref, work, wide, unfolded, corner_vmem, corners, chosen, sem):
    planes = slab_ref.shape[0]
    devices = boxes_ref.shape[0]
    per_row = LANES // BOX_COLS
    box_rows = BOXP * BOX_ROWS // per_row
    corner_at = tasks * box_rows
    numbers = boxes_ref[:, corner_at : corner_at + LOW, :].astype(jnp.float32)[:, 0, :].astype(jnp.int32)
    first = (pltpu.roll(numbers, 1, 1) - slab_number_ref[0]) * planes + numbers
    corner_vmem[...] = jnp.where(iota(numbers.shape, 1) % 4 == 1, first, numbers)
    copy = pltpu.make_async_copy(corner_vmem, corners, sem)
    copy.start()
    work[...] = jnp.zeros_like(work)
    wide[...] = boxes_ref[:, :corner_at, :].astype(jnp.float32).reshape(devices * tasks, box_rows, LANES)
    lane = iota((per_row, LANES), 1)
    copy.wait()

    def look(device, count):
        for task in range(tasks):
            first = corners[device, 4 * task + 1]
            chosen[count] = device * tasks + task
            count += jnp.logical_and(first > -BOXP, first < planes).astype(jnp.int32)
        return count

    count = lax.fori_loop(0, devices, look, 0)
    for extra in range(BATCH):
        chosen[count + extra] = -1

    def add(turn, carry):
        places = []
        for part in range(BATCH):
            index = chosen[turn * BATCH + part]
            box = jnp.maximum(index, 0)
            device, task = box // tasks, box % tasks
            first = jnp.where(index < 0, planes + BOXP - 1, corners[device, 4 * task + 1])
            row, col = corners[device, 4 * task + 2], corners[device, 4 * task + 3]
            places.append((first + BOXP - 1, row))
            inside = jnp.logical_and(lane >= col, lane < col + BOX_COLS)
            rows = wide[box]
            for within in range(per_row):
                turned = rows if within == 0 else pltpu.roll(rows, LANES - within * BOX_COLS, 1)
                unfolded[part, pl.ds(within * box_rows, box_rows), :] = jnp.where(inside, turned, 0.0)
        for part, (plane, row) in enumerate(places):
            for at in range(box_rows):
                tile = unfolded[part, pl.ds(at, per_row, stride=box_rows), :]
                where = pl.ds(row + at % (BOX_ROWS // per_row) * per_row, per_row)
                work[plane + at // (BOX_ROWS // per_row), where, :] += tile
        return carry

    lax.fori_loop(0, (count + BATCH - 1) // BATCH, add, 0)
    slab_ref[...] = work[pl.ds(BOXP - 1, planes)]


def on_device(
    column_blocks,
    onsite,
    neighbor_ids,
    task_atoms,
    chem_shift,
    basis_values,
    box_start,
    box_row,
    box_col,
):
    half = jnp.bfloat16
    holders = lax.axis_size("atoms")
    atoms_here, links, area = column_blocks.shape
    tasks, set_size = task_atoms.shape
    order, points = basis_values.shape[1:]
    blocks = column_blocks.reshape(atoms_here * links, area)

    def side():
        ids, diagonal = lax.optimization_barrier((neighbor_ids, onsite))
        idents = jnp.concatenate([ids % 256, ids // 256], axis=1).astype(half)
        return jnp.concatenate([diagonal, jnp.pad(idents, ((0, 0), (0, area - 2 * links)))], axis=1)

    pieces, extras = gather_columns(blocks, side, holders)
    everything = pl.BlockSpec(memory_space=pl.ANY)
    scalars = pl.BlockSpec(memory_space=pltpu.SMEM)
    vectors = pl.BlockSpec(memory_space=pltpu.VMEM)
    box_rows = (tasks * points // LANES + 1 + 15) // 16 * 16
    density, boxes = pl.pallas_call(
        functools.partial(density_kernel, holders, atoms_here, links),
        in_specs=[scalars] * 4 + [vectors, pl.BlockSpec(memory_space=pltpu.HBM)] + [everything] * (2 * holders),
        out_specs=[everything, vectors],
        out_shape=[
            jax.ShapeDtypeStruct((tasks, order, CENTRAL), half),
            jax.ShapeDtypeStruct((box_rows, LANES), half),
        ],
        scratch_shapes=[
            pltpu.VMEM((holders * atoms_here * links, area), half),
            pltpu.VMEM((holders * atoms_here, 2 * area), half),
            pltpu.VMEM((tasks, order, points), half),
            pltpu.VMEM((tasks, order, CENTRAL), half),
            pltpu.VMEM((tasks * set_size, LOW * links), jnp.float32),
            pltpu.VMEM((tasks * set_size, area), jnp.float32),
            pltpu.VMEM((tasks, 2, LOW * set_size, area), jnp.float32),
            pltpu.VMEM((tasks, order, order), jnp.float32),
            pltpu.VMEM((tasks, set_size), jnp.int32),
            pltpu.SMEM((tasks, set_size), jnp.int32),
            pltpu.SemaphoreType.DMA,
            pltpu.SemaphoreType.DMA((2, holders)),
            pltpu.SemaphoreType.DMA((tasks,)),
            pltpu.SemaphoreType.DMA((tasks,)),
        ],
        compiler_params=pltpu.CompilerParams(vmem_limit_bytes=48 * 1024 * 1024),
    )(
        chem_shift,
        box_start,
        box_row,
        box_col,
        task_atoms,
        basis_values,
        *pieces,
        *extras,
    )
    all_boxes = gather_everywhere(boxes[None])
    slab_number = lax.axis_index("grid").astype(jnp.int32).reshape(1)
    slab = pl.pallas_call(
        functools.partial(slab_kernel, tasks),
        in_specs=[scalars, vectors],
        out_specs=vectors,
        out_shape=jax.ShapeDtypeStruct((PL_SLAB, GRID_ROWS, GRID_COLS), jnp.float32),
        scratch_shapes=[
            pltpu.VMEM((PL_SLAB + 3 * BOXP, GRID_ROWS, GRID_COLS), jnp.float32),
            pltpu.VMEM((all_boxes.shape[0] * tasks, points // LANES, LANES), jnp.float32),
            pltpu.VMEM((BATCH, points // BOX_COLS, LANES), jnp.float32),
            pltpu.VMEM((all_boxes.shape[0], LANES), jnp.int32),
            pltpu.SMEM((all_boxes.shape[0], LANES), jnp.int32),
            pltpu.SMEM((all_boxes.shape[0] * tasks + BATCH,), jnp.int32),
            pltpu.SemaphoreType.DMA,
        ],
        compiler_params=pltpu.CompilerParams(vmem_limit_bytes=32 * 1024 * 1024),
    )(slab_number, all_boxes)
    return density, slab


def solution(mesh):
    placed = (
        P("atoms", None, None),
        P("atoms", None),
        P("atoms", None),
        P(("atoms", "grid"), None),
        P(("atoms", "grid")),
        P(("atoms", "grid"), None, None),
        P(("atoms", "grid")),
        P(("atoms", "grid")),
        P(("atoms", "grid")),
    )
    return jax.shard_map(
        on_device,
        mesh=mesh,
        in_specs=placed,
        out_specs=(P(("atoms", "grid"), None, None), P("grid", None, None)),
        check_vma=False,
    )
```

```python
import functools

import jax
import jax.numpy as jnp
from jax import lax
from jax.experimental import pallas as pl
from jax.experimental.pallas import tpu as pltpu
from jax.sharding import PartitionSpec as P

BS = 16
ITERS = 3
BOXP = 4
BOX_ROWS = 16
BOX_COLS = 16
GRID_ROWS = 32
GRID_COLS = 128
PL_SLAB = 64
CENTRAL = 128

LOW = 8
LANES = 128
BATCH = 4
STAGGER = 1


def power_of_two(size):
    return size & (size - 1) == 0


def gather_everywhere(value):
    for axis in ("grid", "atoms"):
        size = lax.axis_size(axis)
        if not power_of_two(size):
            value = lax.all_gather(value, axis, axis=0, tiled=True)
            continue
        steps = [1 << bit for bit in range(size.bit_length() - 1)][::-1]
        for stage, step in enumerate(steps):
            pairs = [(i, i ^ step) for i in range(size)]
            if axis == "atoms" and step > 1:
                pairs = [(i, i ^ (steps[len(steps) - 2 - stage] if i & 1 else step)) for i in range(size)]
            value = jnp.concatenate([value, lax.ppermute(value, axis, pairs)], axis=0)
    return value


def split(number, size):
    if power_of_two(size):
        return number >> (size.bit_length() - 1), number & (size - 1)
    return number // size, number % size


def slot_of(holder, holders):
    if holders < 2 or not power_of_two(holders):
        return holder
    stages = holders.bit_length() - 2
    apart = holder ^ lax.axis_index("atoms")
    plain = apart >> 1
    turned = sum((((plain >> bit) & 1) << (stages - 1 - bit) for bit in range(stages)), 0 * plain)
    return (apart & 1) * (holders // 2) + jnp.where(holder & 1 == 1, turned, plain)


def gather_columns(blocks, side, holders):
    if holders < 2 or not power_of_two(holders):
        gathered = [lax.all_gather(part, "atoms", axis=0) for part in (blocks, side())]
        return [[whole[i] for i in range(holders)] for whole in gathered]
    stages = holders.bit_length() - 2

    def bit_of(device, stage):
        return 2 << (stages - 1 - stage if device & 1 else stage)

    pairs = [[(i, i ^ bit_of(i, stage)) for i in range(holders)] for stage in range(stages)]
    swap = [(i, i ^ 1) for i in range(holders)]

    def send(part, ways):
        return [lax.ppermute(part, "atoms", pair) for pair in ways]

    def forward(part, firsts):
        have = [part]
        for first, pair in zip(firsts, pairs):
            have = have + [first] + [lax.ppermute(piece, "atoms", pair) for piece in have[1:]]
        return have

    firsts = send(blocks, pairs[:1])
    beside = lax.ppermute(blocks, "atoms", swap)
    beside, wanted = lax.optimization_barrier((beside, side()))
    later, wanted = lax.optimization_barrier((blocks, wanted))
    firsts = firsts + send(later, pairs[1:])
    side_firsts = send(wanted, pairs)
    have = forward(blocks, firsts)
    if stages:
        have[1], side_firsts = lax.optimization_barrier((have[1], side_firsts))
    side_have = forward(wanted, side_firsts)
    swapped = [beside] + [lax.ppermute(piece, "atoms", swap) for piece in have[1:-1]]
    side_swapped = [lax.ppermute(piece, "atoms", swap) for piece in side_have[:-1]]
    mine = jnp.concatenate([blocks, wanted[:, : blocks.shape[1]]], axis=0)
    have[-1], side_have[-1], swapped, side_swapped, mine = lax.optimization_barrier(
        (have[-1], side_have[-1], swapped, side_swapped, mine)
    )
    if stages:
        swapped.append(lax.ppermute(have[-1], "atoms", swap))
    side_swapped.append(lax.ppermute(side_have[-1], "atoms", swap))
    return [[mine] + have[1:] + swapped, side_have + side_swapped]


def iota(shape, axis):
    return lax.broadcasted_iota(jnp.int32, shape, axis)


def nn(left, right):
    return jnp.dot(left, right, preferred_element_type=jnp.float32)


def nt(left, right):
    return lax.dot_general(left, right, (((1,), (1,)), ((), ())), preferred_element_type=jnp.float32)


def plus_diagonal(value, scale, amount):
    here = iota((LANES, LANES), 0) == iota((LANES, LANES), 1)
    diagonal = jnp.where(here, amount, 0.0)
    rows, columns = value.shape
    out = []
    for row in range(0, rows, LANES):
        part = scale * value[row : row + LANES]
        if row < columns:
            pieces = [part[:, :row], part[:, row : row + LANES] + diagonal, part[:, row + LANES :]]
            part = jnp.concatenate([piece for piece in pieces if piece.shape[1]], axis=1)
        out.append(part)
    return jnp.concatenate(out, axis=0)


def density_kernel(
    holders,
    atoms_here,
    links,
    shift_ref,
    start_ref,
    row_ref,
    col_ref,
    members_ref,
    basis_hbm,
    *rest,
):
    pieces, extras = rest[:holders], rest[holders : 2 * holders]
    (
        density_hbm,
        box_ref,
        cols,
        sides,
        basis,
        density,
        ids_all,
        onsite_all,
        product,
        matrix,
        place_vmem,
        place_ref,
        place_sem,
        sems,
        basis_sems,
        density_sems,
    ) = rest[2 * holders :]
    half = jnp.bfloat16
    tasks, set_size = members_ref.shape
    order = set_size * BS
    area = BS * BS
    block_rows = atoms_here * links
    groups = set_size // LOW

    copies = []
    for kind, (parts, whole, count) in enumerate(((extras, sides, atoms_here), (pieces, cols, block_rows))):
        for number, part in enumerate(parts):
            target = whole.at[pl.ds(number * count, count)]
            copies.append(pltpu.make_async_copy(part.at[pl.ds(0, count)], target, sems.at[kind, number]))
    loads = [pltpu.make_async_copy(basis_hbm.at[t], basis.at[t], basis_sems.at[t]) for t in range(tasks)]
    stores = [pltpu.make_async_copy(density.at[t], density_hbm.at[t], density_sems.at[t]) for t in range(tasks)]
    for copy in copies:
        copy.start()
    held_by, held_at = split(members_ref[...], atoms_here)
    slots = slot_of(held_by, holders) * atoms_here + held_at
    place_vmem[...] = slots
    place_copy = pltpu.make_async_copy(place_vmem, place_ref, place_sem)
    place_copy.start()
    for copy in copies[:holders]:
        copy.wait()
    atoms = iota((set_size, holders * atoms_here), 1).astype(jnp.float32)
    diagonal = iota((set_size, set_size), 0) == iota((set_size, set_size), 1)

    def column(rows, task):
        row = rows[task : task + 1].astype(jnp.float32)
        return jnp.sum(jnp.where(diagonal, row, 0.0), axis=1, keepdims=True)

    members = [column(members_ref[...], task) for task in range(tasks)]
    chosen = jnp.concatenate(
        [(column(slots, task) == atoms).astype(jnp.float32) for task in range(tasks)], axis=0
    ).astype(half)
    onsite_all[...] = nn(chosen, sides[:, :area])
    raw = nn(chosen, sides[:, area:]).astype(half)
    source, target = iota((area, LOW * links), 0), iota((area, LOW * links), 1) % links
    spread = jnp.where(source == target, 1.0, jnp.where(source == links + target, 256.0, 0.0)).astype(half)
    ids_all[...] = nn(raw, spread)
    place_copy.wait()
    for copy in copies[holders:]:
        copy.wait()
    for load in loads:
        load.start()

    source, target = iota((area, area), 0), iota((area, area), 1)
    wanted = ((target // LANES) * LOW + target % LOW) * BS + (target % LANES) // LOW
    reorder = (source == wanted).astype(jnp.float32).astype(half)
    side = 2 * LANES if order % (2 * LANES) == 0 else LANES
    identity = (iota((side, side), 0) == iota((side, side), 1)).astype(jnp.float32).astype(half)
    source, target = iota((LANES, LANES), 0), iota((LANES, LANES), 1)
    back = (source == (target % BS) * LOW + target // BS).astype(jnp.float32).astype(half)
    front = (target == (source % BS) * LOW + source // BS).astype(jnp.float32).astype(half)

    lane_owner = iota((LOW, LOW * links), 1) // links
    own = lane_owner == iota((LOW, LOW * links), 0)
    owner_wide = iota((set_size, LOW * links), 1) // links
    lane = iota((set_size, LANES), 1)
    boxes = {}

    def assemble(task, group):
        base = task * set_size + group * LOW
        ids_row = jnp.sum(jnp.where(own, ids_all[pl.ds(base, LOW), :], 0.0), axis=0, keepdims=True)
        match = (members[task] == ids_row).astype(jnp.float32)
        spread_match = jnp.concatenate(
            [jnp.where(owner_wide == low, match, 0.0).astype(half) for low in range(LOW)], axis=0
        )
        stacked = jnp.concatenate(
            [
                cols[pl.ds(pl.multiple_of(place_ref[task, group * LOW + low] * links, links), links), :]
                for low in range(LOW)
            ],
            axis=0,
        )
        spot = product.at[task, group % 2]
        spot[...] = nn(spread_match, stacked)
        for low in range(LOW):
            row = low * set_size + group * LOW + low
            spot[pl.ds(row, 1), :] = onsite_all[pl.ds(base + low, 1), :]
        ordered = nn(spot[...].astype(half), reorder)
        for high in range(area // LANES):
            tiles = [
                ordered[low * set_size : (low + 1) * set_size, high * LANES : (high + 1) * LANES] for low in range(LOW)
            ]
            for step in (1, 2, 4):
                keep = (lane & step) == 0
                for low in range(LOW):
                    if low & step:
                        continue
                    first, second = tiles[low], tiles[low | step]
                    tiles[low] = jnp.where(keep, first, pltpu.roll(second, step, 1))
                    tiles[low | step] = jnp.where(keep, pltpu.roll(first, LANES - step, 1), second)
            for low in range(LOW):
                for upper in range(set_size // LOW):
                    matrix[
                        task,
                        pl.ds(upper * LANES + (high * LOW + low) * LOW, LOW),
                        pl.ds(group * LANES, LANES),
                    ] = tiles[low][upper * LOW : (upper + 1) * LOW]

    def steps_of(task):
        for group in range(groups):
            assemble(task, group)
            yield
        plain = matrix[task].astype(half)
        mirrored = jnp.concatenate(
            [
                jnp.concatenate(
                    [nt(identity, plain[low : low + side, at : at + side]) for low in range(0, order, side)], axis=1
                )
                for at in range(0, order, side)
            ],
            axis=0,
        )
        yield
        whole = plus_diagonal(matrix[task] + mirrored, 0.5, -shift_ref[task])
        bound = jnp.max(jnp.sum(jnp.abs(whole), axis=0, keepdims=True), axis=1, keepdims=True) + 1e-06
        iterate = (whole * (1.0 / bound)).astype(half)
        yield
        for _ in range(ITERS - 1):
            factor = plus_diagonal(nn(iterate, iterate), -0.5, 1.5).astype(half)
            yield
            iterate = nn(iterate, factor).astype(half)
            yield
        factor = plus_diagonal(nn(iterate, iterate[:, :CENTRAL]), -0.5, 1.5).astype(half)
        yield
        turned = plus_diagonal(nn(iterate, factor), -0.5, 0.5).astype(half)
        yield
        mid = nn(turned, back).astype(half)
        tall = nt(front, turned).astype(half)
        wide = []
        for upper in range(order // LANES):
            part = slice(upper * LANES, (upper + 1) * LANES)
            density[task, part, :] = nn(front, mid[part]).astype(half)
            wide.append(nn(tall[:, part], back).astype(half))
        stores[task].start()
        yield
        loads[task].wait()
        weights = nn(jnp.concatenate(wide, axis=1), basis[task])
        values = jnp.sum(weights * basis[task, :CENTRAL, :].astype(jnp.float32), axis=0, keepdims=True)
        rows = values.shape[1] // LANES
        box = jnp.concatenate([values[:, row * LANES : (row + 1) * LANES] for row in range(rows)], axis=0)
        boxes[task] = pltpu.roll(box, col_ref[task], 1)
        yield

    running = []
    waiting = [steps_of(task) for task in range(tasks)]
    tick = 0
    while running or waiting:
        if waiting and tick % STAGGER == 0:
            running.append(waiting.pop(0))
        for steps in list(running):
            if next(steps, running) is running:
                running.remove(steps)
        tick += 1

    lane = iota((1, LANES), 1)
    corner = jnp.zeros((1, LANES), jnp.float32)
    for task in range(tasks):
        numbers = (start_ref[task] // PL_SLAB, start_ref[task] % PL_SLAB, row_ref[task], col_ref[task])
        for place, number in enumerate(numbers):
            corner = jnp.where(lane == task * len(numbers) + place, number.astype(jnp.float32), corner)
    box_rows = [boxes[task] for task in range(tasks)]
    rest_rows = box_ref.shape[0] - sum(box.shape[0] for box in box_rows) - 1
    box_ref[...] = jnp.concatenate(
        box_rows + [corner, jnp.zeros((rest_rows, LANES), jnp.float32)], axis=0
    ).astype(half)
    for store in stores:
        store.wait()


def slab_kernel(tasks, slab_number_ref, boxes_ref, slab_ref, work, wide, unfolded, corner_vmem, corners, chosen, sem):
    planes = slab_ref.shape[0]
    devices = boxes_ref.shape[0]
    per_row = LANES // BOX_COLS
    box_rows = BOXP * BOX_ROWS // per_row
    corner_at = tasks * box_rows
    numbers = boxes_ref[:, corner_at : corner_at + LOW, :].astype(jnp.float32)[:, 0, :].astype(jnp.int32)
    first = (pltpu.roll(numbers, 1, 1) - slab_number_ref[0]) * planes + numbers
    corner_vmem[...] = jnp.where(iota(numbers.shape, 1) % 4 == 1, first, numbers)
    copy = pltpu.make_async_copy(corner_vmem, corners, sem)
    copy.start()
    work[...] = jnp.zeros_like(work)
    wide[...] = boxes_ref[:, :corner_at, :].astype(jnp.float32).reshape(devices * tasks, box_rows, LANES)
    lane = iota((per_row, LANES), 1)
    copy.wait()

    def look(device, count):
        for task in range(tasks):
            first = corners[device, 4 * task + 1]
            chosen[count] = device * tasks + task
            count += jnp.logical_and(first > -BOXP, first < planes).astype(jnp.int32)
        return count

    count = lax.fori_loop(0, devices, look, 0)
    for extra in range(BATCH):
        chosen[count + extra] = -1

    def add(turn, carry):
        places = []
        for part in range(BATCH):
            index = chosen[turn * BATCH + part]
            box = jnp.maximum(index, 0)
            device, task = box // tasks, box % tasks
            first = jnp.where(index < 0, planes + BOXP - 1, corners[device, 4 * task + 1])
            row, col = corners[device, 4 * task + 2], corners[device, 4 * task + 3]
            places.append((first + BOXP - 1, row))
            inside = jnp.logical_and(lane >= col, lane < col + BOX_COLS)
            rows = wide[box]
            for within in range(per_row):
                turned = rows if within == 0 else pltpu.roll(rows, LANES - within * BOX_COLS, 1)
                unfolded[part, pl.ds(within * box_rows, box_rows), :] = jnp.where(inside, turned, 0.0)
        for part, (plane, row) in enumerate(places):
            for at in range(box_rows):
                tile = unfolded[part, pl.ds(at, per_row, stride=box_rows), :]
                where = pl.ds(row + at % (BOX_ROWS // per_row) * per_row, per_row)
                work[plane + at // (BOX_ROWS // per_row), where, :] += tile
        return carry

    lax.fori_loop(0, (count + BATCH - 1) // BATCH, add, 0)
    slab_ref[...] = work[pl.ds(BOXP - 1, planes)]


def on_device(
    column_blocks,
    onsite,
    neighbor_ids,
    task_atoms,
    chem_shift,
    basis_values,
    box_start,
    box_row,
    box_col,
):
    half = jnp.bfloat16
    holders = lax.axis_size("atoms")
    atoms_here, links, area = column_blocks.shape
    tasks, set_size = task_atoms.shape
    order, points = basis_values.shape[1:]
    blocks = column_blocks.reshape(atoms_here * links, area)

    def side():
        ids, diagonal = lax.optimization_barrier((neighbor_ids, onsite))
        idents = jnp.concatenate([ids % 256, ids // 256], axis=1).astype(half)
        return jnp.concatenate([diagonal, jnp.pad(idents, ((0, 0), (0, area - 2 * links)))], axis=1)

    pieces, extras = gather_columns(blocks, side, holders)
    everything = pl.BlockSpec(memory_space=pl.ANY)
    scalars = pl.BlockSpec(memory_space=pltpu.SMEM)
    vectors = pl.BlockSpec(memory_space=pltpu.VMEM)
    box_rows = (tasks * points // LANES + 1 + 15) // 16 * 16
    density, boxes = pl.pallas_call(
        functools.partial(density_kernel, holders, atoms_here, links),
        in_specs=[scalars] * 4 + [vectors, pl.BlockSpec(memory_space=pltpu.HBM)] + [everything] * (2 * holders),
        out_specs=[everything, vectors],
        out_shape=[
            jax.ShapeDtypeStruct((tasks, order, CENTRAL), half),
            jax.ShapeDtypeStruct((box_rows, LANES), half),
        ],
        scratch_shapes=[
            pltpu.VMEM((holders * atoms_here * links, area), half),
            pltpu.VMEM((holders * atoms_here, 2 * area), half),
            pltpu.VMEM((tasks, order, points), half),
            pltpu.VMEM((tasks, order, CENTRAL), half),
            pltpu.VMEM((tasks * set_size, LOW * links), jnp.float32),
            pltpu.VMEM((tasks * set_size, area), jnp.float32),
            pltpu.VMEM((tasks, 2, LOW * set_size, area), jnp.float32),
            pltpu.VMEM((tasks, order, order), jnp.float32),
            pltpu.VMEM((tasks, set_size), jnp.int32),
            pltpu.SMEM((tasks, set_size), jnp.int32),
            pltpu.SemaphoreType.DMA,
            pltpu.SemaphoreType.DMA((2, holders)),
            pltpu.SemaphoreType.DMA((tasks,)),
            pltpu.SemaphoreType.DMA((tasks,)),
        ],
        compiler_params=pltpu.CompilerParams(vmem_limit_bytes=48 * 1024 * 1024),
    )(
        chem_shift,
        box_start,
        box_row,
        box_col,
        task_atoms,
        basis_values,
        *pieces,
        *extras,
    )
    all_boxes = gather_everywhere(boxes[None])
    slab_number = lax.axis_index("grid").astype(jnp.int32).reshape(1)
    slab = pl.pallas_call(
        functools.partial(slab_kernel, tasks),
        in_specs=[scalars, vectors],
        out_specs=vectors,
        out_shape=jax.ShapeDtypeStruct((PL_SLAB, GRID_ROWS, GRID_COLS), jnp.float32),
        scratch_shapes=[
            pltpu.VMEM((PL_SLAB + 3 * BOXP, GRID_ROWS, GRID_COLS), jnp.float32),
            pltpu.VMEM((all_boxes.shape[0] * tasks, points // LANES, LANES), jnp.float32),
            pltpu.VMEM((BATCH, points // BOX_COLS, LANES), jnp.float32),
            pltpu.VMEM((all_boxes.shape[0], LANES), jnp.int32),
            pltpu.SMEM((all_boxes.shape[0], LANES), jnp.int32),
            pltpu.SMEM((all_boxes.shape[0] * tasks + BATCH,), jnp.int32),
            pltpu.SemaphoreType.DMA,
        ],
        compiler_params=pltpu.CompilerParams(vmem_limit_bytes=32 * 1024 * 1024),
    )(slab_number, all_boxes)
    return density, slab


def solution(mesh):
    placed = (
        P("atoms", None, None),
        P("atoms", None),
        P("atoms", None),
        P(("atoms", "grid"), None),
        P(("atoms", "grid")),
        P(("atoms", "grid"), None, None),
        P(("atoms", "grid")),
        P(("atoms", "grid")),
        P(("atoms", "grid")),
    )
    return jax.shard_map(
        on_device,
        mesh=mesh,
        in_specs=placed,
        out_specs=(P(("atoms", "grid"), None, None), P("grid", None, None)),
        check_vma=False,
    )
```

```python
import functools

import jax
import jax.numpy as jnp
from jax import lax
from jax.experimental import pallas as pl
from jax.experimental.pallas import tpu as pltpu
from jax.sharding import PartitionSpec as P

BS = 16
ITERS = 3
BOXP = 4
BOX_ROWS = 16
BOX_COLS = 16
GRID_ROWS = 32
GRID_COLS = 128
PL_SLAB = 64
CENTRAL = 128

LOW = 8
LANES = 128
BATCH = 4
STAGGER = 1


def power_of_two(size):
    return size & (size - 1) == 0


def gather_everywhere(value):
    for axis in ("grid", "atoms"):
        size = lax.axis_size(axis)
        if not power_of_two(size):
            value = lax.all_gather(value, axis, axis=0, tiled=True)
            continue
        steps = [1 << bit for bit in range(size.bit_length() - 1)][::-1]
        for stage, step in enumerate(steps):
            pairs = [(i, i ^ step) for i in range(size)]
            value = jnp.concatenate([value, lax.ppermute(value, axis, pairs)], axis=0)
    return value


def split(number, size):
    if power_of_two(size):
        return number >> (size.bit_length() - 1), number & (size - 1)
    return number // size, number % size


def slot_of(holder, holders):
    if holders < 2 or not power_of_two(holders):
        return holder
    stages = holders.bit_length() - 2
    apart = holder ^ lax.axis_index("atoms")
    plain = apart >> 1
    turned = sum((((plain >> bit) & 1) << (stages - 1 - bit) for bit in range(stages)), 0 * plain)
    return (apart & 1) * (holders // 2) + jnp.where(holder & 1 == 1, turned, plain)


def gather_columns(blocks, side, holders):
    if holders < 2 or not power_of_two(holders):
        gathered = [lax.all_gather(part, "atoms", axis=0) for part in (blocks, side())]
        return [[whole[i] for i in range(holders)] for whole in gathered]
    stages = holders.bit_length() - 2

    def bit_of(device, stage):
        return 2 << (stages - 1 - stage if device & 1 else stage)

    pairs = [[(i, i ^ bit_of(i, stage)) for i in range(holders)] for stage in range(stages)]
    swap = [(i, i ^ 1) for i in range(holders)]

    def send(part, ways):
        return [lax.ppermute(part, "atoms", pair) for pair in ways]

    def forward(part, firsts):
        have = [part]
        for first, pair in zip(firsts, pairs):
            have = have + [first] + [lax.ppermute(piece, "atoms", pair) for piece in have[1:]]
        return have

    firsts = send(blocks, pairs[:1])
    beside = lax.ppermute(blocks, "atoms", swap)
    beside, wanted = lax.optimization_barrier((beside, side()))
    later, wanted = lax.optimization_barrier((blocks, wanted))
    firsts = firsts + send(later, pairs[1:])
    side_firsts = send(wanted, pairs)
    have = forward(blocks, firsts)
    if stages:
        have[1], side_firsts = lax.optimization_barrier((have[1], side_firsts))
    side_have = forward(wanted, side_firsts)
    swapped = [beside] + [lax.ppermute(piece, "atoms", swap) for piece in have[1:-1]]
    side_swapped = [lax.ppermute(piece, "atoms", swap) for piece in side_have[:-1]]
    mine = jnp.concatenate([blocks, wanted[:, : blocks.shape[1]]], axis=0)
    have[-1], side_have[-1], swapped, side_swapped, mine = lax.optimization_barrier(
        (have[-1], side_have[-1], swapped, side_swapped, mine)
    )
    if stages:
        swapped.append(lax.ppermute(have[-1], "atoms", swap))
    side_swapped.append(lax.ppermute(side_have[-1], "atoms", swap))
    return [[mine] + have[1:] + swapped, side_have + side_swapped]


def iota(shape, axis):
    return lax.broadcasted_iota(jnp.int32, shape, axis)


def nn(left, right):
    return jnp.dot(left, right, preferred_element_type=jnp.float32)


def nt(left, right):
    return lax.dot_general(left, right, (((1,), (1,)), ((), ())), preferred_element_type=jnp.float32)


def plus_diagonal(value, scale, amount):
    here = iota((LANES, LANES), 0) == iota((LANES, LANES), 1)
    diagonal = jnp.where(here, amount, 0.0)
    rows, columns = value.shape
    out = []
    for row in range(0, rows, LANES):
        part = scale * value[row : row + LANES]
        if row < columns:
            pieces = [part[:, :row], part[:, row : row + LANES] + diagonal, part[:, row + LANES :]]
            part = jnp.concatenate([piece for piece in pieces if piece.shape[1]], axis=1)
        out.append(part)
    return jnp.concatenate(out, axis=0)


def density_kernel(
    holders,
    atoms_here,
    links,
    shift_ref,
    start_ref,
    row_ref,
    col_ref,
    members_ref,
    basis_hbm,
    *rest,
):
    pieces, extras = rest[:holders], rest[holders : 2 * holders]
    (
        density,
        box_ref,
        cols,
        sides,
        basis,
        ids_all,
        onsite_all,
        product,
        matrix,
        place_vmem,
        place_ref,
        place_sem,
        sems,
        basis_sems,
    ) = rest[2 * holders :]
    half = jnp.bfloat16
    tasks, set_size = members_ref.shape
    order = set_size * BS
    area = BS * BS
    block_rows = atoms_here * links
    groups = set_size // LOW

    copies = []
    for kind, (parts, whole, count) in enumerate(((extras, sides, atoms_here), (pieces, cols, block_rows))):
        for number, part in enumerate(parts):
            target = whole.at[pl.ds(number * count, count)]
            copies.append(pltpu.make_async_copy(part.at[pl.ds(0, count)], target, sems.at[kind, number]))
    loads = [pltpu.make_async_copy(basis_hbm.at[t], basis.at[t], basis_sems.at[t]) for t in range(tasks)]
    for copy in copies:
        copy.start()
    held_by, held_at = split(members_ref[...], atoms_here)
    slots = slot_of(held_by, holders) * atoms_here + held_at
    place_vmem[...] = slots
    place_copy = pltpu.make_async_copy(place_vmem, place_ref, place_sem)
    place_copy.start()
    for copy in copies[:holders]:
        copy.wait()
    atoms = iota((set_size, holders * atoms_here), 1).astype(jnp.float32)
    diagonal = iota((set_size, set_size), 0) == iota((set_size, set_size), 1)

    def column(rows, task):
        row = rows[task : task + 1].astype(jnp.float32)
        return jnp.sum(jnp.where(diagonal, row, 0.0), axis=1, keepdims=True)

    members = [column(members_ref[...], task) for task in range(tasks)]
    chosen = jnp.concatenate(
        [(column(slots, task) == atoms).astype(jnp.float32) for task in range(tasks)], axis=0
    ).astype(half)
    onsite_all[...] = nn(chosen, sides[:, :area])
    raw = nn(chosen, sides[:, area:]).astype(half)
    source, target = iota((area, LOW * links), 0), iota((area, LOW * links), 1) % links
    spread = jnp.where(source == target, 1.0, jnp.where(source == links + target, 256.0, 0.0)).astype(half)
    ids_all[...] = nn(raw, spread)
    place_copy.wait()
    for copy in copies[holders:]:
        copy.wait()
    for load in loads:
        load.start()

    source, target = iota((area, area), 0), iota((area, area), 1)
    wanted = ((target // LANES) * LOW + target % LOW) * BS + (target % LANES) // LOW
    reorder = (source == wanted).astype(jnp.float32).astype(half)
    side = 2 * LANES if order % (2 * LANES) == 0 else LANES
    identity = (iota((side, side), 0) == iota((side, side), 1)).astype(jnp.float32).astype(half)
    source, target = iota((LANES, LANES), 0), iota((LANES, LANES), 1)
    back = (source == (target % BS) * LOW + target // BS).astype(jnp.float32).astype(half)
    front = (target == (source % BS) * LOW + source // BS).astype(jnp.float32).astype(half)

    lane_owner = iota((LOW, LOW * links), 1) // links
    own = lane_owner == iota((LOW, LOW * links), 0)
    owner_wide = iota((set_size, LOW * links), 1) // links
    lane = iota((set_size, LANES), 1)
    boxes = {}

    def assemble(task, group):
        base = task * set_size + group * LOW
        ids_row = jnp.sum(jnp.where(own, ids_all[pl.ds(base, LOW), :], 0.0), axis=0, keepdims=True)
        match = (members[task] == ids_row).astype(jnp.float32)
        spread_match = jnp.concatenate(
            [jnp.where(owner_wide == low, match, 0.0).astype(half) for low in range(LOW)], axis=0
        )
        stacked = jnp.concatenate(
            [
                cols[pl.ds(pl.multiple_of(place_ref[task, group * LOW + low] * links, links), links), :]
                for low in range(LOW)
            ],
            axis=0,
        )
        spot = product.at[task, group % 2]
        spot[...] = nn(spread_match, stacked)
        for low in range(LOW):
            row = low * set_size + group * LOW + low
            spot[pl.ds(row, 1), :] = onsite_all[pl.ds(base + low, 1), :]
        yield
        ordered = nn(spot[...].astype(half), reorder)
        for high in range(area // LANES):
            tiles = [
                ordered[low * set_size : (low + 1) * set_size, high * LANES : (high + 1) * LANES] for low in range(LOW)
            ]
            for step in (1, 2, 4):
                keep = (lane & step) == 0
                for low in range(LOW):
                    if low & step:
                        continue
                    first, second = tiles[low], tiles[low | step]
                    tiles[low] = jnp.where(keep, first, pltpu.roll(second, step, 1))
                    tiles[low | step] = jnp.where(keep, pltpu.roll(first, LANES - step, 1), second)
            for low in range(LOW):
                for upper in range(set_size // LOW):
                    matrix[
                        task,
                        pl.ds(upper * LANES + (high * LOW + low) * LOW, LOW),
                        pl.ds(group * LANES, LANES),
                    ] = tiles[low][upper * LOW : (upper + 1) * LOW]

    def steps_of(task):
        for group in range(groups):
            yield from assemble(task, group)
            yield
        plain = matrix[task].astype(half)
        mirrored = jnp.concatenate(
            [
                jnp.concatenate(
                    [nt(identity, plain[low : low + side, at : at + side]) for low in range(0, order, side)], axis=1
                )
                for at in range(0, order, side)
            ],
            axis=0,
        )
        yield
        whole = plus_diagonal(matrix[task] + mirrored, 0.5, -shift_ref[task])
        bound = jnp.max(jnp.sum(jnp.abs(whole), axis=0, keepdims=True), axis=1, keepdims=True) + 1e-06
        iterate = (whole * (1.0 / bound)).astype(half)
        yield
        for _ in range(ITERS - 1):
            factor = plus_diagonal(nn(iterate, iterate), -0.5, 1.5).astype(half)
            yield
            iterate = nn(iterate, factor).astype(half)
            yield
        factor = plus_diagonal(nn(iterate, iterate[:, :CENTRAL]), -0.5, 1.5).astype(half)
        yield
        turned = plus_diagonal(nn(iterate, factor), -0.5, 0.5).astype(half)
        yield
        mid = nn(turned, back).astype(half)
        tall = nt(front, turned).astype(half)
        wide = []
        for upper in range(order // LANES):
            part = slice(upper * LANES, (upper + 1) * LANES)
            density[task, part, :] = nn(front, mid[part]).astype(half)
            wide.append(nn(tall[:, part], back).astype(half))
        yield
        if task == 0:
            for load in loads:
                load.wait()
        weights = nn(jnp.concatenate(wide, axis=1), basis[task])
        yield
        values = jnp.sum(weights * basis[task, :CENTRAL, :].astype(jnp.float32), axis=0, keepdims=True)
        rows = values.shape[1] // LANES
        box = jnp.concatenate([values[:, row * LANES : (row + 1) * LANES] for row in range(rows)], axis=0)
        boxes[task] = pltpu.roll(box, col_ref[task], 1)
        yield

    running = []
    waiting = [steps_of(task) for task in range(tasks)]
    tick = 0
    while running or waiting:
        if waiting and tick % STAGGER == 0:
            running.append(waiting.pop(0))
        for steps in list(running):
            if next(steps, running) is running:
                running.remove(steps)
        tick += 1

    lane = iota((1, LANES), 1)
    corner = jnp.zeros((1, LANES), jnp.float32)
    for task in range(tasks):
        numbers = (start_ref[task] // PL_SLAB, start_ref[task] % PL_SLAB, row_ref[task], col_ref[task])
        for place, number in enumerate(numbers):
            corner = jnp.where(lane == task * len(numbers) + place, number.astype(jnp.float32), corner)
    box_rows = [boxes[task] for task in range(tasks)]
    rest_rows = box_ref.shape[0] - sum(box.shape[0] for box in box_rows) - 1
    box_ref[...] = jnp.concatenate(
        box_rows + [corner, jnp.zeros((rest_rows, LANES), jnp.float32)], axis=0
    ).astype(half)


def slab_kernel(tasks, slab_number_ref, boxes_ref, slab_ref, work, wide, unfolded, corner_vmem, corners, chosen, sem):
    planes = slab_ref.shape[0]
    devices = boxes_ref.shape[0]
    per_row = LANES // BOX_COLS
    box_rows = BOXP * BOX_ROWS // per_row
    corner_at = tasks * box_rows
    numbers = boxes_ref[:, corner_at : corner_at + LOW, :].astype(jnp.float32)[:, 0, :].astype(jnp.int32)
    first = (pltpu.roll(numbers, 1, 1) - slab_number_ref[0]) * planes + numbers
    corner_vmem[...] = jnp.where(iota(numbers.shape, 1) % 4 == 1, first, numbers)
    copy = pltpu.make_async_copy(corner_vmem, corners, sem)
    copy.start()
    work[...] = jnp.zeros_like(work)
    wide[...] = boxes_ref[:, :corner_at, :].astype(jnp.float32).reshape(devices * tasks, box_rows, LANES)
    lane = iota((per_row, LANES), 1)
    copy.wait()

    def look(device, count):
        for task in range(tasks):
            first = corners[device, 4 * task + 1]
            chosen[count] = device * tasks + task
            count += jnp.logical_and(first > -BOXP, first < planes).astype(jnp.int32)
        return count

    count = lax.fori_loop(0, devices, look, 0, unroll=4 if devices % 4 == 0 else 1)
    for extra in range(BATCH):
        chosen[count + extra] = -1

    def add(turn, carry):
        places = []
        for part in range(BATCH):
            index = chosen[turn * BATCH + part]
            box = jnp.maximum(index, 0)
            device, task = box // tasks, box % tasks
            first = jnp.where(index < 0, planes + BOXP - 1, corners[device, 4 * task + 1])
            row, col = corners[device, 4 * task + 2], corners[device, 4 * task + 3]
            places.append((first + BOXP - 1, row))
            inside = jnp.logical_and(lane >= col, lane < col + BOX_COLS)
            rows = wide[box]
            for within in range(per_row):
                turned = rows if within == 0 else pltpu.roll(rows, LANES - within * BOX_COLS, 1)
                unfolded[part, pl.ds(within * box_rows, box_rows), :] = jnp.where(inside, turned, 0.0)
        for part, (plane, row) in enumerate(places):
            for at in range(box_rows):
                tile = unfolded[part, pl.ds(at, per_row, stride=box_rows), :]
                where = pl.ds(row + at % (BOX_ROWS // per_row) * per_row, per_row)
                work[plane + at // (BOX_ROWS // per_row), where, :] += tile
        return carry

    lax.fori_loop(0, (count + BATCH - 1) // BATCH, add, 0)
    slab_ref[...] = work[pl.ds(BOXP - 1, planes)]


def on_device(
    column_blocks,
    onsite,
    neighbor_ids,
    task_atoms,
    chem_shift,
    basis_values,
    box_start,
    box_row,
    box_col,
):
    half = jnp.bfloat16
    holders = lax.axis_size("atoms")
    atoms_here, links, area = column_blocks.shape
    tasks, set_size = task_atoms.shape
    order, points = basis_values.shape[1:]
    blocks = column_blocks.reshape(atoms_here * links, area)

    def side():
        ids, diagonal = lax.optimization_barrier((neighbor_ids, onsite))
        idents = jnp.concatenate([ids % 256, ids // 256], axis=1).astype(half)
        return jnp.concatenate([diagonal, jnp.pad(idents, ((0, 0), (0, area - 2 * links)))], axis=1)

    pieces, extras = gather_columns(blocks, side, holders)
    everything = pl.BlockSpec(memory_space=pl.ANY)
    scalars = pl.BlockSpec(memory_space=pltpu.SMEM)
    vectors = pl.BlockSpec(memory_space=pltpu.VMEM)
    box_rows = (tasks * points // LANES + 1 + 15) // 16 * 16
    density, boxes = pl.pallas_call(
        functools.partial(density_kernel, holders, atoms_here, links),
        in_specs=[scalars] * 4 + [vectors, pl.BlockSpec(memory_space=pltpu.HBM)] + [everything] * (2 * holders),
        out_specs=[vectors, vectors],
        out_shape=[
            jax.ShapeDtypeStruct((tasks, order, CENTRAL), half),
            jax.ShapeDtypeStruct((box_rows, LANES), half),
        ],
        scratch_shapes=[
            pltpu.VMEM((holders * atoms_here * links, area), half),
            pltpu.VMEM((holders * atoms_here, 2 * area), half),
            pltpu.VMEM((tasks, order, points), half),
            pltpu.VMEM((tasks * set_size, LOW * links), jnp.float32),
            pltpu.VMEM((tasks * set_size, area), jnp.float32),
            pltpu.VMEM((tasks, 2, LOW * set_size, area), jnp.float32),
            pltpu.VMEM((tasks, order, order), jnp.float32),
            pltpu.VMEM((tasks, set_size), jnp.int32),
            pltpu.SMEM((tasks, set_size), jnp.int32),
            pltpu.SemaphoreType.DMA,
            pltpu.SemaphoreType.DMA((2, holders)),
            pltpu.SemaphoreType.DMA((tasks,)),
        ],
        compiler_params=pltpu.CompilerParams(vmem_limit_bytes=48 * 1024 * 1024),
    )(
        chem_shift,
        box_start,
        box_row,
        box_col,
        task_atoms,
        basis_values,
        *pieces,
        *extras,
    )
    all_boxes = gather_everywhere(boxes[None])
    slab_number = lax.axis_index("grid").astype(jnp.int32).reshape(1)
    slab = pl.pallas_call(
        functools.partial(slab_kernel, tasks),
        in_specs=[scalars, vectors],
        out_specs=vectors,
        out_shape=jax.ShapeDtypeStruct((PL_SLAB, GRID_ROWS, GRID_COLS), jnp.float32),
        scratch_shapes=[
            pltpu.VMEM((PL_SLAB + 3 * BOXP, GRID_ROWS, GRID_COLS), jnp.float32),
            pltpu.VMEM((all_boxes.shape[0] * tasks, points // LANES, LANES), jnp.float32),
            pltpu.VMEM((BATCH, points // BOX_COLS, LANES), jnp.float32),
            pltpu.VMEM((all_boxes.shape[0], LANES), jnp.int32),
            pltpu.SMEM((all_boxes.shape[0], LANES), jnp.int32),
            pltpu.SMEM((all_boxes.shape[0] * tasks + BATCH,), jnp.int32),
            pltpu.SemaphoreType.DMA,
        ],
        compiler_params=pltpu.CompilerParams(vmem_limit_bytes=32 * 1024 * 1024),
    )(slab_number, all_boxes)
    return density, slab


def solution(mesh):
    placed = (
        P("atoms", None, None),
        P("atoms", None),
        P("atoms", None),
        P(("atoms", "grid"), None),
        P(("atoms", "grid")),
        P(("atoms", "grid"), None, None),
        P(("atoms", "grid")),
        P(("atoms", "grid")),
        P(("atoms", "grid")),
    )
    return jax.shard_map(
        on_device,
        mesh=mesh,
        in_specs=placed,
        out_specs=(P(("atoms", "grid"), None, None), P("grid", None, None)),
        check_vma=False,
    )
```

```python
import functools

import jax
import jax.numpy as jnp
from jax import lax
from jax.experimental import pallas as pl
from jax.experimental.pallas import tpu as pltpu
from jax.sharding import PartitionSpec as P

BS = 16
ITERS = 3
BOXP = 4
BOX_ROWS = 16
BOX_COLS = 16
GRID_ROWS = 32
GRID_COLS = 128
PL_SLAB = 64
CENTRAL = 128

LOW = 8
LANES = 128
BATCH = 8
STAGGER = 1


def power_of_two(size):
    return size & (size - 1) == 0


def gather_everywhere(value):
    for axis in ("grid", "atoms"):
        size = lax.axis_size(axis)
        if not power_of_two(size):
            value = lax.all_gather(value, axis, axis=0, tiled=True)
            continue
        steps = [1 << bit for bit in range(size.bit_length() - 1)][::-1]
        for stage, step in enumerate(steps):
            pairs = [(i, i ^ step) for i in range(size)]
            value = jnp.concatenate([value, lax.ppermute(value, axis, pairs)], axis=0)
    return value


def split(number, size):
    if power_of_two(size):
        return number >> (size.bit_length() - 1), number & (size - 1)
    return number // size, number % size


def slot_of(holder, holders):
    if holders < 2 or not power_of_two(holders):
        return holder
    stages = holders.bit_length() - 2
    apart = holder ^ lax.axis_index("atoms")
    plain = apart >> 1
    turned = sum((((plain >> bit) & 1) << (stages - 1 - bit) for bit in range(stages)), 0 * plain)
    return (apart & 1) * (holders // 2) + jnp.where(holder & 1 == 1, turned, plain)


def gather_columns(blocks, side, holders):
    if holders < 2 or not power_of_two(holders):
        gathered = [lax.all_gather(part, "atoms", axis=0) for part in (blocks, side())]
        return [[whole[i] for i in range(holders)] for whole in gathered]
    stages = holders.bit_length() - 2

    def bit_of(device, stage):
        return 2 << (stages - 1 - stage if device & 1 else stage)

    pairs = [[(i, i ^ bit_of(i, stage)) for i in range(holders)] for stage in range(stages)]
    swap = [(i, i ^ 1) for i in range(holders)]

    def send(part, ways):
        return [lax.ppermute(part, "atoms", pair) for pair in ways]

    def forward(part, firsts):
        have = [part]
        for first, pair in zip(firsts, pairs):
            have = have + [first] + [lax.ppermute(piece, "atoms", pair) for piece in have[1:]]
        return have

    firsts = send(blocks, pairs[:1])
    beside = lax.ppermute(blocks, "atoms", swap)
    beside, wanted = lax.optimization_barrier((beside, side()))
    mine = jnp.concatenate([blocks, wanted[:, : blocks.shape[1]]], axis=0)
    later, wanted, mine = lax.optimization_barrier((blocks, wanted, mine))
    firsts = firsts + send(later, pairs[1:])
    side_firsts = send(wanted, pairs)
    have = forward(blocks, firsts)
    if stages:
        have[1], side_firsts = lax.optimization_barrier((have[1], side_firsts))
    side_have = forward(wanted, side_firsts)
    swapped = [beside] + [lax.ppermute(piece, "atoms", swap) for piece in have[1:-1]]
    side_swapped = [lax.ppermute(piece, "atoms", swap) for piece in side_have[:-1]]
    have[-1], side_have[-1], swapped, side_swapped = lax.optimization_barrier(
        (have[-1], side_have[-1], swapped, side_swapped)
    )
    if stages:
        swapped.append(lax.ppermute(have[-1], "atoms", swap))
    side_swapped.append(lax.ppermute(side_have[-1], "atoms", swap))
    return [[mine] + have[1:] + swapped, side_have + side_swapped]


def iota(shape, axis):
    return lax.broadcasted_iota(jnp.int32, shape, axis)


def nn(left, right):
    return jnp.dot(left, right, preferred_element_type=jnp.float32)


def nt(left, right):
    return lax.dot_general(left, right, (((1,), (1,)), ((), ())), preferred_element_type=jnp.float32)


def plus_diagonal(value, scale, amount):
    here = iota((LANES, LANES), 0) == iota((LANES, LANES), 1)
    diagonal = jnp.where(here, amount, 0.0)
    rows, columns = value.shape
    out = []
    for row in range(0, rows, LANES):
        part = scale * value[row : row + LANES]
        if row < columns:
            pieces = [part[:, :row], part[:, row : row + LANES] + diagonal, part[:, row + LANES :]]
            part = jnp.concatenate([piece for piece in pieces if piece.shape[1]], axis=1)
        out.append(part)
    return jnp.concatenate(out, axis=0)


def density_kernel(
    holders,
    atoms_here,
    links,
    shift_ref,
    start_ref,
    row_ref,
    col_ref,
    members_ref,
    basis_hbm,
    *rest,
):
    pieces, extras = rest[:holders], rest[holders : 2 * holders]
    (
        density,
        box_ref,
        cols,
        sides,
        basis,
        ids_all,
        onsite_all,
        product,
        matrix,
        place_vmem,
        place_ref,
        place_sem,
        sems,
        basis_sems,
    ) = rest[2 * holders :]
    half = jnp.bfloat16
    tasks, set_size = members_ref.shape
    order = set_size * BS
    area = BS * BS
    block_rows = atoms_here * links
    groups = set_size // LOW

    copies = []
    for kind, (parts, whole, count) in enumerate(((extras, sides, atoms_here), (pieces, cols, block_rows))):
        for number, part in enumerate(parts):
            target = whole.at[pl.ds(number * count, count)]
            copies.append(pltpu.make_async_copy(part.at[pl.ds(0, count)], target, sems.at[kind, number]))
    loads = [pltpu.make_async_copy(basis_hbm.at[t], basis.at[t], basis_sems.at[t]) for t in range(tasks)]
    for copy in copies:
        copy.start()
    held_by, held_at = split(members_ref[...], atoms_here)
    slots = slot_of(held_by, holders) * atoms_here + held_at
    place_vmem[...] = slots
    place_copy = pltpu.make_async_copy(place_vmem, place_ref, place_sem)
    place_copy.start()
    for copy in copies[:holders]:
        copy.wait()
    atoms = iota((set_size, holders * atoms_here), 1).astype(jnp.float32)
    diagonal = iota((set_size, set_size), 0) == iota((set_size, set_size), 1)

    def column(rows, task):
        row = rows[task : task + 1].astype(jnp.float32)
        return jnp.sum(jnp.where(diagonal, row, 0.0), axis=1, keepdims=True)

    members = [column(members_ref[...], task) for task in range(tasks)]
    chosen = jnp.concatenate(
        [(column(slots, task) == atoms).astype(jnp.float32) for task in range(tasks)], axis=0
    ).astype(half)
    onsite_all[...] = nn(chosen, sides[:, :area])
    raw = nn(chosen, sides[:, area:]).astype(half)
    source, target = iota((area, LOW * links), 0), iota((area, LOW * links), 1) % links
    spread = jnp.where(source == target, 1.0, jnp.where(source == links + target, 256.0, 0.0)).astype(half)
    ids_all[...] = nn(raw, spread)
    place_copy.wait()
    for copy in copies[holders:]:
        copy.wait()
    for load in loads:
        load.start()

    source, target = iota((area, area), 0), iota((area, area), 1)
    wanted = ((target // LANES) * LOW + target % LOW) * BS + (target % LANES) // LOW
    reorder = (source == wanted).astype(jnp.float32).astype(half)
    side = 2 * LANES if order % (2 * LANES) == 0 else LANES
    identity = (iota((side, side), 0) == iota((side, side), 1)).astype(jnp.float32).astype(half)
    source, target = iota((LANES, LANES), 0), iota((LANES, LANES), 1)
    back = (source == (target % BS) * LOW + target // BS).astype(jnp.float32).astype(half)
    front = (target == (source % BS) * LOW + source // BS).astype(jnp.float32).astype(half)

    lane_owner = iota((LOW, LOW * links), 1) // links
    own = lane_owner == iota((LOW, LOW * links), 0)
    owner_wide = iota((set_size, LOW * links), 1) // links
    lane = iota((set_size, LANES), 1)
    boxes = {}

    def assemble(task, group):
        base = task * set_size + group * LOW
        ids_row = jnp.sum(jnp.where(own, ids_all[pl.ds(base, LOW), :], 0.0), axis=0, keepdims=True)
        match = (members[task] == ids_row).astype(jnp.float32)
        spread_match = jnp.concatenate(
            [jnp.where(owner_wide == low, match, 0.0).astype(half) for low in range(LOW)], axis=0
        )
        stacked = jnp.concatenate(
            [
                cols[pl.ds(pl.multiple_of(place_ref[task, group * LOW + low] * links, links), links), :]
                for low in range(LOW)
            ],
            axis=0,
        )
        spot = product.at[task, group % 2]
        spot[...] = nn(spread_match, stacked)
        for low in range(LOW):
            row = low * set_size + group * LOW + low
            spot[pl.ds(row, 1), :] = onsite_all[pl.ds(base + low, 1), :]
        yield
        ordered = nn(spot[...].astype(half), reorder)
        for high in range(area // LANES):
            tiles = [
                ordered[low * set_size : (low + 1) * set_size, high * LANES : (high + 1) * LANES] for low in range(LOW)
            ]
            for step in (1, 2, 4):
                keep = (lane & step) == 0
                for low in range(LOW):
                    if low & step:
                        continue
                    first, second = tiles[low], tiles[low | step]
                    tiles[low] = jnp.where(keep, first, pltpu.roll(second, step, 1))
                    tiles[low | step] = jnp.where(keep, pltpu.roll(first, LANES - step, 1), second)
            for low in range(LOW):
                for upper in range(set_size // LOW):
                    matrix[
                        task,
                        pl.ds(upper * LANES + (high * LOW + low) * LOW, LOW),
                        pl.ds(group * LANES, LANES),
                    ] = tiles[low][upper * LOW : (upper + 1) * LOW]

    def steps_of(task):
        for group in range(groups):
            yield from assemble(task, group)
            yield
        plain = matrix[task].astype(half)
        mirrored = jnp.concatenate(
            [
                jnp.concatenate(
                    [nt(identity, plain[low : low + side, at : at + side]) for low in range(0, order, side)], axis=1
                )
                for at in range(0, order, side)
            ],
            axis=0,
        )
        yield
        whole = plus_diagonal(matrix[task] + mirrored, 0.5, -shift_ref[task])
        bound = jnp.max(jnp.sum(jnp.abs(whole), axis=0, keepdims=True), axis=1, keepdims=True) + 1e-06
        iterate = (whole * (1.0 / bound)).astype(half)
        yield
        for _ in range(ITERS - 1):
            factor = plus_diagonal(nn(iterate, iterate), -0.5, 1.5).astype(half)
            yield
            iterate = nn(iterate, factor).astype(half)
            yield
        factor = plus_diagonal(nn(iterate, iterate[:, :CENTRAL]), -0.5, 1.5).astype(half)
        yield
        turned = plus_diagonal(nn(iterate, factor), -0.5, 0.5).astype(half)
        yield
        mid = nn(turned, back).astype(half)
        tall = nt(front, turned).astype(half)
        wide = []
        for upper in range(order // LANES):
            part = slice(upper * LANES, (upper + 1) * LANES)
            density[task, part, :] = nn(front, mid[part]).astype(half)
            wide.append(nn(tall[:, part], back).astype(half))
        yield
        if task == 0:
            for load in loads:
                load.wait()
        weights = nn(jnp.concatenate(wide, axis=1), basis[task])
        yield
        values = jnp.sum(weights * basis[task, :CENTRAL, :].astype(jnp.float32), axis=0, keepdims=True)
        rows = values.shape[1] // LANES
        box = jnp.concatenate([values[:, row * LANES : (row + 1) * LANES] for row in range(rows)], axis=0)
        boxes[task] = pltpu.roll(box, col_ref[task], 1)
        yield

    running = []
    waiting = [steps_of(task) for task in range(tasks)]
    tick = 0
    while running or waiting:
        if waiting and tick % STAGGER == 0:
            running.append(waiting.pop(0))
        for steps in list(running):
            if next(steps, running) is running:
                running.remove(steps)
        tick += 1

    lane = iota((1, LANES), 1)
    corner = jnp.zeros((1, LANES), jnp.float32)
    for task in range(tasks):
        numbers = (start_ref[task] // PL_SLAB, start_ref[task] % PL_SLAB, row_ref[task], col_ref[task])
        for place, number in enumerate(numbers):
            corner = jnp.where(lane == task * len(numbers) + place, number.astype(jnp.float32), corner)
    box_rows = [boxes[task] for task in range(tasks)]
    rest_rows = box_ref.shape[0] - sum(box.shape[0] for box in box_rows) - 1
    box_ref[...] = jnp.concatenate(
        box_rows + [corner, jnp.zeros((rest_rows, LANES), jnp.float32)], axis=0
    ).astype(half)


def slab_kernel(tasks, slab_number_ref, boxes_ref, slab_ref, work, wide, unfolded, corner_vmem, corners, chosen, sem):
    planes = slab_ref.shape[0]
    devices = boxes_ref.shape[0]
    per_row = LANES // BOX_COLS
    box_rows = BOXP * BOX_ROWS // per_row
    corner_at = tasks * box_rows
    numbers = boxes_ref[:, corner_at : corner_at + LOW, :].astype(jnp.float32)[:, 0, :].astype(jnp.int32)
    first = (pltpu.roll(numbers, 1, 1) - slab_number_ref[0]) * planes + numbers
    corner_vmem[...] = jnp.where(iota(numbers.shape, 1) % 4 == 1, first, numbers)
    copy = pltpu.make_async_copy(corner_vmem, corners, sem)
    copy.start()
    work[...] = jnp.zeros_like(work)
    wide[...] = boxes_ref[:, :corner_at, :].astype(jnp.float32).reshape(devices * tasks, box_rows, LANES)
    lane = iota((per_row, LANES), 1)
    copy.wait()

    def look(device, count):
        for task in range(tasks):
            first = corners[device, 4 * task + 1]
            chosen[count] = device * tasks + task
            count += jnp.logical_and(first > -BOXP, first < planes).astype(jnp.int32)
        return count

    count = lax.fori_loop(0, devices, look, 0, unroll=4 if devices % 4 == 0 else 1)
    for extra in range(BATCH):
        chosen[count + extra] = -1

    def add(turn, carry):
        places = []
        for part in range(BATCH):
            index = chosen[turn * BATCH + part]
            box = jnp.maximum(index, 0)
            device, task = box // tasks, box % tasks
            first = jnp.where(index < 0, planes + BOXP - 1, corners[device, 4 * task + 1])
            row, col = corners[device, 4 * task + 2], corners[device, 4 * task + 3]
            places.append((first + BOXP - 1, row))
            inside = jnp.logical_and(lane >= col, lane < col + BOX_COLS)
            rows = wide[box]
            for within in range(per_row):
                turned = rows if within == 0 else pltpu.roll(rows, LANES - within * BOX_COLS, 1)
                unfolded[part, pl.ds(within * box_rows, box_rows), :] = jnp.where(inside, turned, 0.0)
        for part, (plane, row) in enumerate(places):
            for at in range(box_rows):
                tile = unfolded[part, pl.ds(at, per_row, stride=box_rows), :]
                where = pl.ds(row + at % (BOX_ROWS // per_row) * per_row, per_row)
                work[plane + at // (BOX_ROWS // per_row), where, :] += tile
        return carry

    lax.fori_loop(0, (count + BATCH - 1) // BATCH, add, 0)
    slab_ref[...] = work[pl.ds(BOXP - 1, planes)]


def on_device(
    column_blocks,
    onsite,
    neighbor_ids,
    task_atoms,
    chem_shift,
    basis_values,
    box_start,
    box_row,
    box_col,
):
    half = jnp.bfloat16
    holders = lax.axis_size("atoms")
    atoms_here, links, area = column_blocks.shape
    tasks, set_size = task_atoms.shape
    order, points = basis_values.shape[1:]
    blocks = column_blocks.reshape(atoms_here * links, area)

    def side():
        ids, diagonal = lax.optimization_barrier((neighbor_ids, onsite))
        idents = jnp.concatenate([ids % 256, ids // 256], axis=1).astype(half)
        return jnp.concatenate([diagonal, jnp.pad(idents, ((0, 0), (0, area - 2 * links)))], axis=1)

    pieces, extras = gather_columns(blocks, side, holders)
    everything = pl.BlockSpec(memory_space=pl.ANY)
    scalars = pl.BlockSpec(memory_space=pltpu.SMEM)
    vectors = pl.BlockSpec(memory_space=pltpu.VMEM)
    box_rows = (tasks * points // LANES + 1 + 15) // 16 * 16
    density, boxes = pl.pallas_call(
        functools.partial(density_kernel, holders, atoms_here, links),
        in_specs=[scalars] * 4 + [vectors, pl.BlockSpec(memory_space=pltpu.HBM)] + [everything] * (2 * holders),
        out_specs=[vectors, vectors],
        out_shape=[
            jax.ShapeDtypeStruct((tasks, order, CENTRAL), half),
            jax.ShapeDtypeStruct((box_rows, LANES), half),
        ],
        scratch_shapes=[
            pltpu.VMEM((holders * atoms_here * links, area), half),
            pltpu.VMEM((holders * atoms_here, 2 * area), half),
            pltpu.VMEM((tasks, order, points), half),
            pltpu.VMEM((tasks * set_size, LOW * links), jnp.float32),
            pltpu.VMEM((tasks * set_size, area), jnp.float32),
            pltpu.VMEM((tasks, 2, LOW * set_size, area), jnp.float32),
            pltpu.VMEM((tasks, order, order), jnp.float32),
            pltpu.VMEM((tasks, set_size), jnp.int32),
            pltpu.SMEM((tasks, set_size), jnp.int32),
            pltpu.SemaphoreType.DMA,
            pltpu.SemaphoreType.DMA((2, holders)),
            pltpu.SemaphoreType.DMA((tasks,)),
        ],
        compiler_params=pltpu.CompilerParams(vmem_limit_bytes=48 * 1024 * 1024),
    )(
        chem_shift,
        box_start,
        box_row,
        box_col,
        task_atoms,
        basis_values,
        *pieces,
        *extras,
    )
    all_boxes = gather_everywhere(boxes[None])
    slab_number = lax.axis_index("grid").astype(jnp.int32).reshape(1)
    slab = pl.pallas_call(
        functools.partial(slab_kernel, tasks),
        in_specs=[scalars, vectors],
        out_specs=vectors,
        out_shape=jax.ShapeDtypeStruct((PL_SLAB, GRID_ROWS, GRID_COLS), jnp.float32),
        scratch_shapes=[
            pltpu.VMEM((PL_SLAB + 3 * BOXP, GRID_ROWS, GRID_COLS), jnp.float32),
            pltpu.VMEM((all_boxes.shape[0] * tasks, points // LANES, LANES), jnp.float32),
            pltpu.VMEM((BATCH, points // BOX_COLS, LANES), jnp.float32),
            pltpu.VMEM((all_boxes.shape[0], LANES), jnp.int32),
            pltpu.SMEM((all_boxes.shape[0], LANES), jnp.int32),
            pltpu.SMEM((all_boxes.shape[0] * tasks + BATCH,), jnp.int32),
            pltpu.SemaphoreType.DMA,
        ],
        compiler_params=pltpu.CompilerParams(vmem_limit_bytes=32 * 1024 * 1024),
    )(slab_number, all_boxes)
    return density, slab


def solution(mesh):
    placed = (
        P("atoms", None, None),
        P("atoms", None),
        P("atoms", None),
        P(("atoms", "grid"), None),
        P(("atoms", "grid")),
        P(("atoms", "grid"), None, None),
        P(("atoms", "grid")),
        P(("atoms", "grid")),
        P(("atoms", "grid")),
    )
    return jax.shard_map(
        on_device,
        mesh=mesh,
        in_specs=placed,
        out_specs=(P(("atoms", "grid"), None, None), P("grid", None, None)),
        check_vma=False,
    )
```

```python
import functools

import jax
import jax.numpy as jnp
from jax import lax
from jax.experimental import pallas as pl
from jax.experimental.pallas import tpu as pltpu
from jax.sharding import PartitionSpec as P

BS = 16
ITERS = 3
BOXP = 4
BOX_ROWS = 16
BOX_COLS = 16
GRID_ROWS = 32
GRID_COLS = 128
PL_SLAB = 64
CENTRAL = 128

LOW = 8
LANES = 128
BATCH = 8
STAGGER = 1


def power_of_two(size):
    return size & (size - 1) == 0


def gather_everywhere(value):
    for axis in ("grid", "atoms"):
        size = lax.axis_size(axis)
        if not power_of_two(size):
            value = lax.all_gather(value, axis, axis=0, tiled=True)
            continue
        steps = [1 << bit for bit in range(size.bit_length() - 1)][::-1]
        for stage, step in enumerate(steps):
            pairs = [(i, i ^ step) for i in range(size)]
            value = jnp.concatenate([value, lax.ppermute(value, axis, pairs)], axis=0)
    return value


def split(number, size):
    if power_of_two(size):
        return number >> (size.bit_length() - 1), number & (size - 1)
    return number // size, number % size


def slot_of(holder, holders):
    if holders < 2 or not power_of_two(holders):
        return holder
    stages = holders.bit_length() - 2
    apart = holder ^ lax.axis_index("atoms")
    plain = apart >> 1
    turned = sum((((plain >> bit) & 1) << (stages - 1 - bit) for bit in range(stages)), 0 * plain)
    return (apart & 1) * (holders // 2) + jnp.where(holder & 1 == 1, turned, plain)


def gather_columns(blocks, side, holders):
    if holders < 2 or not power_of_two(holders):
        gathered = [lax.all_gather(part, "atoms", axis=0) for part in (blocks, side())]
        return [[whole[i] for i in range(holders)] for whole in gathered]
    stages = holders.bit_length() - 2

    def bit_of(device, stage):
        return 2 << (stages - 1 - stage if device & 1 else stage)

    pairs = [[(i, i ^ bit_of(i, stage)) for i in range(holders)] for stage in range(stages)]
    swap = [(i, i ^ 1) for i in range(holders)]

    def send(part, ways):
        return [lax.ppermute(part, "atoms", pair) for pair in ways]

    def forward(part, firsts):
        have = [part]
        for first, pair in zip(firsts, pairs):
            have = have + [first] + [lax.ppermute(piece, "atoms", pair) for piece in have[1:]]
        return have

    firsts = send(blocks, pairs[:1])
    beside = lax.ppermute(blocks, "atoms", swap)
    beside, wanted = lax.optimization_barrier((beside, side()))
    mine = jnp.concatenate([blocks, wanted[:, : blocks.shape[1]]], axis=0)
    later, wanted, mine = lax.optimization_barrier((blocks, wanted, mine))
    firsts = firsts + send(later, pairs[1:])
    side_firsts = send(wanted, pairs)
    have = forward(blocks, firsts)
    if stages:
        have[1], side_firsts = lax.optimization_barrier((have[1], side_firsts))
    side_have = forward(wanted, side_firsts)
    swapped = [beside] + [lax.ppermute(piece, "atoms", swap) for piece in have[1:-1]]
    side_swapped = [lax.ppermute(piece, "atoms", swap) for piece in side_have[:-1]]
    have[-1], side_have[-1], swapped, side_swapped = lax.optimization_barrier(
        (have[-1], side_have[-1], swapped, side_swapped)
    )
    if stages:
        swapped.append(lax.ppermute(have[-1], "atoms", swap))
    side_swapped.append(lax.ppermute(side_have[-1], "atoms", swap))
    return [[mine] + have[1:] + swapped, side_have + side_swapped]


def iota(shape, axis):
    return lax.broadcasted_iota(jnp.int32, shape, axis)


def nn(left, right):
    return jnp.dot(left, right, preferred_element_type=jnp.float32)


def nt(left, right):
    return lax.dot_general(left, right, (((1,), (1,)), ((), ())), preferred_element_type=jnp.float32)


def plus_diagonal(value, scale, amount):
    here = iota((LANES, LANES), 0) == iota((LANES, LANES), 1)
    diagonal = jnp.where(here, amount, 0.0)
    rows, columns = value.shape
    out = []
    for row in range(0, rows, LANES):
        part = scale * value[row : row + LANES]
        if row < columns:
            pieces = [part[:, :row], part[:, row : row + LANES] + diagonal, part[:, row + LANES :]]
            part = jnp.concatenate([piece for piece in pieces if piece.shape[1]], axis=1)
        out.append(part)
    return jnp.concatenate(out, axis=0)


def density_kernel(
    holders,
    atoms_here,
    links,
    shift_ref,
    start_ref,
    row_ref,
    col_ref,
    members_ref,
    basis_hbm,
    *rest,
):
    pieces, extras = rest[:holders], rest[holders : 2 * holders]
    (
        density,
        box_ref,
        cols,
        sides,
        basis,
        ids_all,
        onsite_all,
        product,
        matrix,
        place_vmem,
        place_ref,
        place_sem,
        sems,
        basis_sems,
    ) = rest[2 * holders :]
    half = jnp.bfloat16
    tasks, set_size = members_ref.shape
    order = set_size * BS
    area = BS * BS
    block_rows = atoms_here * links
    groups = set_size // LOW

    copies = []
    for kind, (parts, whole, count) in enumerate(((extras, sides, atoms_here), (pieces, cols, block_rows))):
        for number, part in enumerate(parts):
            target = whole.at[pl.ds(number * count, count)]
            copies.append(pltpu.make_async_copy(part.at[pl.ds(0, count)], target, sems.at[kind, number]))
    loads = [pltpu.make_async_copy(basis_hbm.at[t], basis.at[t], basis_sems.at[t]) for t in range(tasks)]
    for copy in copies:
        copy.start()
    held_by, held_at = split(members_ref[...], atoms_here)
    slots = slot_of(held_by, holders) * atoms_here + held_at
    place_vmem[...] = slots
    place_copy = pltpu.make_async_copy(place_vmem, place_ref, place_sem)
    place_copy.start()
    for copy in copies[:holders]:
        copy.wait()
    atoms = iota((set_size, holders * atoms_here), 1).astype(jnp.float32)
    diagonal = iota((set_size, set_size), 0) == iota((set_size, set_size), 1)

    def column(rows, task):
        row = rows[task : task + 1].astype(jnp.float32)
        return jnp.sum(jnp.where(diagonal, row, 0.0), axis=1, keepdims=True)

    members = [column(members_ref[...], task) for task in range(tasks)]
    chosen = jnp.concatenate(
        [(column(slots, task) == atoms).astype(jnp.float32) for task in range(tasks)], axis=0
    ).astype(half)
    onsite_all[...] = nn(chosen, sides[:, :area])
    raw = nn(chosen, sides[:, area:]).astype(half)
    wide = (raw.shape[1], LOW * links)
    source, target = iota(wide, 0), iota(wide, 1) % links
    spread = jnp.where(source == target, 1.0, jnp.where(source == links + target, 256.0, 0.0)).astype(half)
    ids_all[...] = nn(raw, spread)
    place_copy.wait()
    for copy in copies[holders:]:
        copy.wait()
    for load in loads:
        load.start()

    source, target = iota((area, area), 0), iota((area, area), 1)
    wanted = ((target // LANES) * LOW + target % LOW) * BS + (target % LANES) // LOW
    reorder = (source == wanted).astype(jnp.float32).astype(half)
    side = 2 * LANES if order % (2 * LANES) == 0 else LANES
    identity = (iota((side, side), 0) == iota((side, side), 1)).astype(jnp.float32).astype(half)
    source, target = iota((LANES, LANES), 0), iota((LANES, LANES), 1)
    back = (source == (target % BS) * LOW + target // BS).astype(jnp.float32).astype(half)
    front = (target == (source % BS) * LOW + source // BS).astype(jnp.float32).astype(half)

    lane_owner = iota((LOW, LOW * links), 1) // links
    own = lane_owner == iota((LOW, LOW * links), 0)
    owner_wide = iota((set_size, LOW * links), 1) // links
    lane = iota((set_size, LANES), 1)
    boxes = {}

    def assemble(task, group):
        base = task * set_size + group * LOW
        ids_row = jnp.sum(jnp.where(own, ids_all[pl.ds(base, LOW), :], 0.0), axis=0, keepdims=True)
        match = (members[task] == ids_row).astype(jnp.float32)
        spread_match = jnp.concatenate(
            [jnp.where(owner_wide == low, match, 0.0).astype(half) for low in range(LOW)], axis=0
        )
        stacked = jnp.concatenate(
            [
                cols[pl.ds(pl.multiple_of(place_ref[task, group * LOW + low] * links, links), links), :]
                for low in range(LOW)
            ],
            axis=0,
        )
        spot = product.at[task, group % 2]
        spot[...] = nn(spread_match, stacked)
        for low in range(LOW):
            row = low * set_size + group * LOW + low
            spot[pl.ds(row, 1), :] = onsite_all[pl.ds(base + low, 1), :]
        yield
        ordered = nn(spot[...].astype(half), reorder)
        for high in range(area // LANES):
            tiles = [
                ordered[low * set_size : (low + 1) * set_size, high * LANES : (high + 1) * LANES] for low in range(LOW)
            ]
            for step in (1, 2, 4):
                keep = (lane & step) == 0
                for low in range(LOW):
                    if low & step:
                        continue
                    first, second = tiles[low], tiles[low | step]
                    tiles[low] = jnp.where(keep, first, pltpu.roll(second, step, 1))
                    tiles[low | step] = jnp.where(keep, pltpu.roll(first, LANES - step, 1), second)
            for low in range(LOW):
                for upper in range(set_size // LOW):
                    matrix[
                        task,
                        pl.ds(upper * LANES + (high * LOW + low) * LOW, LOW),
                        pl.ds(group * LANES, LANES),
                    ] = tiles[low][upper * LOW : (upper + 1) * LOW]

    def steps_of(task):
        for group in range(groups):
            yield from assemble(task, group)
            yield
        plain = matrix[task].astype(half)
        mirrored = jnp.concatenate(
            [
                jnp.concatenate(
                    [nt(identity, plain[low : low + side, at : at + side]) for low in range(0, order, side)], axis=1
                )
                for at in range(0, order, side)
            ],
            axis=0,
        )
        yield
        whole = plus_diagonal(matrix[task] + mirrored, 0.5, -shift_ref[task])
        bound = jnp.max(jnp.sum(jnp.abs(whole), axis=0, keepdims=True), axis=1, keepdims=True) + 1e-06
        iterate = (whole * (1.0 / bound)).astype(half)
        yield
        for _ in range(ITERS - 1):
            factor = plus_diagonal(nn(iterate, iterate), -0.5, 1.5).astype(half)
            yield
            iterate = nn(iterate, factor).astype(half)
            yield
        factor = plus_diagonal(nn(iterate, iterate[:, :CENTRAL]), -0.5, 1.5).astype(half)
        yield
        turned = plus_diagonal(nn(iterate, factor), -0.5, 0.5).astype(half)
        yield
        mid = nn(turned, back).astype(half)
        tall = nt(front, turned).astype(half)
        wide = []
        for upper in range(order // LANES):
            part = slice(upper * LANES, (upper + 1) * LANES)
            density[task, part, :] = nn(front, mid[part]).astype(half)
            wide.append(nn(tall[:, part], back).astype(half))
        yield
        if task == 0:
            for load in loads:
                load.wait()
        weights = nn(jnp.concatenate(wide, axis=1), basis[task])
        yield
        values = jnp.sum(weights * basis[task, :CENTRAL, :].astype(jnp.float32), axis=0, keepdims=True)
        rows = values.shape[1] // LANES
        box = jnp.concatenate([values[:, row * LANES : (row + 1) * LANES] for row in range(rows)], axis=0)
        boxes[task] = pltpu.roll(box, col_ref[task], 1)
        yield

    running = []
    waiting = [steps_of(task) for task in range(tasks)]
    tick = 0
    while running or waiting:
        if waiting and tick % STAGGER == 0:
            running.append(waiting.pop(0))
        for steps in list(running):
            if next(steps, running) is running:
                running.remove(steps)
        tick += 1

    lane = iota((1, LANES), 1)
    corner = jnp.zeros((1, LANES), jnp.float32)
    for task in range(tasks):
        numbers = (start_ref[task] // PL_SLAB, start_ref[task] % PL_SLAB, row_ref[task], col_ref[task])
        for place, number in enumerate(numbers):
            corner = jnp.where(lane == task * len(numbers) + place, number.astype(jnp.float32), corner)
    box_rows = [boxes[task] for task in range(tasks)]
    rest_rows = box_ref.shape[0] - sum(box.shape[0] for box in box_rows) - 1
    box_ref[...] = jnp.concatenate(
        box_rows + [corner, jnp.zeros((rest_rows, LANES), jnp.float32)], axis=0
    ).astype(half)


def slab_kernel(tasks, slab_number_ref, boxes_ref, slab_ref, work, wide, unfolded, corner_vmem, corners, chosen, sem):
    planes = slab_ref.shape[0]
    devices = boxes_ref.shape[0]
    per_row = LANES // BOX_COLS
    box_rows = BOXP * BOX_ROWS // per_row
    corner_at = tasks * box_rows
    numbers = boxes_ref[:, corner_at : corner_at + LOW, :].astype(jnp.float32)[:, 0, :].astype(jnp.int32)
    first = (pltpu.roll(numbers, 1, 1) - slab_number_ref[0]) * planes + numbers
    corner_vmem[...] = jnp.where(iota(numbers.shape, 1) % 4 == 1, first, numbers)
    copy = pltpu.make_async_copy(corner_vmem, corners, sem)
    copy.start()
    work[...] = jnp.zeros_like(work)
    wide[...] = boxes_ref[:, :corner_at, :].astype(jnp.float32).reshape(devices * tasks, box_rows, LANES)
    lane = iota((per_row, LANES), 1)
    copy.wait()

    def look(device, count):
        for task in range(tasks):
            first = corners[device, 4 * task + 1]
            chosen[count] = device * tasks + task
            count += jnp.logical_and(first > -BOXP, first < planes).astype(jnp.int32)
        return count

    count = lax.fori_loop(0, devices, look, 0, unroll=4 if devices % 4 == 0 else 1)
    for extra in range(BATCH):
        chosen[count + extra] = -1

    def add(turn, carry):
        places = []
        for part in range(BATCH):
            index = chosen[turn * BATCH + part]
            box = jnp.maximum(index, 0)
            device, task = box // tasks, box % tasks
            first = jnp.where(index < 0, planes + BOXP - 1, corners[device, 4 * task + 1])
            row, col = corners[device, 4 * task + 2], corners[device, 4 * task + 3]
            places.append((first + BOXP - 1, row))
            inside = jnp.logical_and(lane >= col, lane < col + BOX_COLS)
            rows = wide[box]
            for within in range(per_row):
                turned = rows if within == 0 else pltpu.roll(rows, LANES - within * BOX_COLS, 1)
                unfolded[part, pl.ds(within * box_rows, box_rows), :] = jnp.where(inside, turned, 0.0)
        for part, (plane, row) in enumerate(places):
            for at in range(box_rows):
                tile = unfolded[part, pl.ds(at, per_row, stride=box_rows), :]
                where = pl.ds(row + at % (BOX_ROWS // per_row) * per_row, per_row)
                work[plane + at // (BOX_ROWS // per_row), where, :] += tile
        return carry

    lax.fori_loop(0, (count + BATCH - 1) // BATCH, add, 0)
    slab_ref[...] = work[pl.ds(BOXP - 1, planes)]


def on_device(
    column_blocks,
    onsite,
    neighbor_ids,
    task_atoms,
    chem_shift,
    basis_values,
    box_start,
    box_row,
    box_col,
):
    half = jnp.bfloat16
    holders = lax.axis_size("atoms")
    atoms_here, links, area = column_blocks.shape
    tasks, set_size = task_atoms.shape
    order, points = basis_values.shape[1:]
    blocks = column_blocks.reshape(atoms_here * links, area)

    def side():
        ids, diagonal = lax.optimization_barrier((neighbor_ids, onsite))
        idents = jnp.concatenate([ids % 256, ids // 256], axis=1).astype(half)
        return jnp.concatenate([diagonal, jnp.pad(idents, ((0, 0), (0, -2 * links % LANES)))], axis=1)

    pieces, extras = gather_columns(blocks, side, holders)
    everything = pl.BlockSpec(memory_space=pl.ANY)
    scalars = pl.BlockSpec(memory_space=pltpu.SMEM)
    vectors = pl.BlockSpec(memory_space=pltpu.VMEM)
    box_rows = tasks * points // LANES + LOW
    density, boxes = pl.pallas_call(
        functools.partial(density_kernel, holders, atoms_here, links),
        in_specs=[scalars] * 4 + [vectors, pl.BlockSpec(memory_space=pltpu.HBM)] + [everything] * (2 * holders),
        out_specs=[vectors, vectors],
        out_shape=[
            jax.ShapeDtypeStruct((tasks, order, CENTRAL), half),
            jax.ShapeDtypeStruct((box_rows, LANES), half),
        ],
        scratch_shapes=[
            pltpu.VMEM((holders * atoms_here * links, area), half),
            pltpu.VMEM((holders * atoms_here, area + (2 * links + LANES - 1) // LANES * LANES), half),
            pltpu.VMEM((tasks, order, points), half),
            pltpu.VMEM((tasks * set_size, LOW * links), jnp.float32),
            pltpu.VMEM((tasks * set_size, area), jnp.float32),
            pltpu.VMEM((tasks, 2, LOW * set_size, area), jnp.float32),
            pltpu.VMEM((tasks, order, order), jnp.float32),
            pltpu.VMEM((tasks, set_size), jnp.int32),
            pltpu.SMEM((tasks, set_size), jnp.int32),
            pltpu.SemaphoreType.DMA,
            pltpu.SemaphoreType.DMA((2, holders)),
            pltpu.SemaphoreType.DMA((tasks,)),
        ],
        compiler_params=pltpu.CompilerParams(vmem_limit_bytes=48 * 1024 * 1024),
    )(
        chem_shift,
        box_start,
        box_row,
        box_col,
        task_atoms,
        basis_values,
        *pieces,
        *extras,
    )
    all_boxes = gather_everywhere(boxes[None])
    slab_number = lax.axis_index("grid").astype(jnp.int32).reshape(1)
    slab = pl.pallas_call(
        functools.partial(slab_kernel, tasks),
        in_specs=[scalars, vectors],
        out_specs=vectors,
        out_shape=jax.ShapeDtypeStruct((PL_SLAB, GRID_ROWS, GRID_COLS), jnp.float32),
        scratch_shapes=[
            pltpu.VMEM((PL_SLAB + 3 * BOXP, GRID_ROWS, GRID_COLS), jnp.float32),
            pltpu.VMEM((all_boxes.shape[0] * tasks, points // LANES, LANES), jnp.float32),
            pltpu.VMEM((BATCH, points // BOX_COLS, LANES), jnp.float32),
            pltpu.VMEM((all_boxes.shape[0], LANES), jnp.int32),
            pltpu.SMEM((all_boxes.shape[0], LANES), jnp.int32),
            pltpu.SMEM((all_boxes.shape[0] * tasks + BATCH,), jnp.int32),
            pltpu.SemaphoreType.DMA,
        ],
        compiler_params=pltpu.CompilerParams(vmem_limit_bytes=32 * 1024 * 1024),
    )(slab_number, all_boxes)
    return density, slab


def solution(mesh):
    placed = (
        P("atoms", None, None),
        P("atoms", None),
        P("atoms", None),
        P(("atoms", "grid"), None),
        P(("atoms", "grid")),
        P(("atoms", "grid"), None, None),
        P(("atoms", "grid")),
        P(("atoms", "grid")),
        P(("atoms", "grid")),
    )
    return jax.shard_map(
        on_device,
        mesh=mesh,
        in_specs=placed,
        out_specs=(P(("atoms", "grid"), None, None), P("grid", None, None)),
        check_vma=False,
    )
```
